512 devices in a mesh: src: 32 (over z, x), dst: 16 (over y, core).
Axes of the slice: x: 4, y: 8, z: 8, core: 2. Of those that a mesh axis runs over, the one named last changes fastest.
Arguments:
- src_table: bfloat16 [16384, 400], P(('src', 'dst')), may hold values from -2.5 to 2.5
- dst_table: bfloat16 [12288, 400], P(('dst', 'src')), may hold values from -2.5 to 2.5
- rel_diag: float32 [512, 400], replicated, may hold values from 0.1 to 1.9
- src_index: int32 [32, 16, 512], P('src', 'dst'), may hold values from 0 to 511
- dst_index: int32 [32, 16, 512], P('src', 'dst'), may hold values from 0 to 767
- rel_index: int32 [32, 16, 512], P('src', 'dst'), may hold values from 0 to 511
- neg_index: int32 [32, 16, 2, 512], P('src', 'dst'), may hold values from 0 to 767
- edge_count: int32 [32, 16], P('src', 'dst'), may hold values from 32 to 512, as said below
Outputs:
- grad_src: float32 [16384, 400], P(('src', 'dst'))
- grad_dst: float32 [12288, 400], P(('dst', 'src'))
- grad_rel: float32 [512, 400], replicated
The draws below stay inside these ranges and needn't reach their ends.
Inputs may be any that keep to these rules, and one draw needn't show every extreme that they name: Edge slots 0 to edge_count[a, b] - 1 of bucket (a, b) are live and the rest are ignored; some bucket has exactly 512 live edges and some has exactly 32.
All inputs are finite; a program needn't handle non-finite values.
Results may differ from the reference program's by a relative error of at most 0.0021.
Values may be sent and summed in bfloat16 or wider, within the bound.
A program may use at most 64 MiB of HBM per device.

```python
import math
import jax
import jax.numpy as jnp
from jax import lax

D = 400
R = 512
E_CAP = 512
CH = 256
NEG = 512
PROWS_S = 512
PROWS_D = 768
SPANS = 2
N_SRC = 32
N_DST = 16


def draw_edge_count(key, part):
    keys = jax.random.split(jax.random.fold_in(key, 7), 4)
    total = N_SRC * N_DST
    shifts = jax.random.randint(keys[0], (total,), 0, 4)
    divisor = jnp.left_shift(jnp.ones((total,), jnp.int32), shifts)
    base = E_CAP // divisor
    lower = jax.random.randint(keys[1], (total,), 0, E_CAP // 16 + 1)
    counts = base - lower
    top_bucket = jax.random.randint(keys[2], (), 0, total)
    low_bucket = (top_bucket + 1 + jax.random.randint(keys[3], (), 0, total - 1)) % total
    counts = counts.at[top_bucket].set(E_CAP).at[low_bucket].set(E_CAP // 16)
    return counts.reshape(N_SRC, N_DST).astype(jnp.int32)


def place_ends(array, key, smallest, high):
    longest = array.shape.index(max(array.shape))
    spots = []
    for shift in (0, 1):
        where = [jax.random.randint(jax.random.fold_in(key, axis), (), 0, length) for axis, length in enumerate(array.shape)]
        where[longest] = (where[longest] + shift) % array.shape[longest]
        spots.append(tuple(where))
    return array.at[spots[0]].set(smallest).at[spots[1]].set(high)


def steps_of(key, extent, pieces, low, largest):
    level, own = 1.0, jax.random.fold_in(key, 6)
    for axis_at, parts in pieces:
        heights = jnp.exp(jax.random.uniform(jax.random.fold_in(own, axis_at), (parts,), jnp.float32, low / len(pieces), largest / len(pieces)))
        level = level * jnp.repeat(heights, extent[axis_at] // parts).reshape([-1 if axis == axis_at else 1 for axis in range(len(extent))])
    return level


def centred(stream_key, shape, scale, reach, shards=(), kind=jnp.bfloat16):
    gain = steps_of(stream_key, shape, shards, -0.22, 0.18) if shards else 1.0
    array = jax.random.normal(stream_key, shape, jnp.float32) * scale * gain
    return jnp.minimum(jnp.maximum(array, -reach), reach).astype(kind)


def setup_inputs(seed: int = 0) -> dict:
    splits = jax.random.split(jax.random.key(seed), 9)
    src_table = centred(splits[0], (N_SRC * PROWS_S, D), 0.35, 2.5, ((0, 512),))
    dst_table = centred(splits[1], (N_DST * PROWS_D, D), 0.35, 2.5, ((0, 512),))
    rel_diag = jnp.clip(1.0 + 0.18 * jax.random.normal(splits[2], (R, D), jnp.float32), 0.1, 1.9)
    src_index = place_ends(jax.random.randint(splits[3], (N_SRC, N_DST, E_CAP), 0, PROWS_S), jax.random.fold_in(splits[3], 1), 0, PROWS_S - 1).astype(jnp.int32)
    dst_index = place_ends(jax.random.randint(splits[4], (N_SRC, N_DST, E_CAP), 0, PROWS_D), jax.random.fold_in(splits[4], 1), 0, PROWS_D - 1).astype(jnp.int32)
    rel_index = place_ends(jax.random.randint(splits[5], (N_SRC, N_DST, E_CAP), 0, R), jax.random.fold_in(splits[5], 1), 0, R - 1).astype(jnp.int32)
    neg_index = place_ends(jax.random.randint(splits[6], (N_SRC, N_DST, SPANS, NEG), 0, PROWS_D), jax.random.fold_in(splits[6], 1), 0, PROWS_D - 1).astype(jnp.int32)
    edge_count = draw_edge_count(jax.random.fold_in(splits[8], 71), 0)
    return {"src_table": src_table, "dst_table": dst_table, "rel_diag": rel_diag, "src_index": src_index, "dst_index": dst_index, "rel_index": rel_index, "neg_index": neg_index, "edge_count": edge_count}


def bucket_terms(source_part, target_part, rel_diag, source_rows, target_rows, relation_rows, negative_rows, live_count):
    inverse = 1.0 / math.sqrt(NEG)
    live_mask = (jnp.arange(E_CAP, dtype=jnp.int32) < live_count).astype(jnp.float32)
    source_vec = jnp.take(source_part, source_rows, axis=0).astype(jnp.float32)
    target_vec = jnp.take(target_part, target_rows, axis=0).astype(jnp.float32)
    relation_vec = jnp.take(rel_diag, relation_rows, axis=0)
    scaled = source_vec * relation_vec
    rounded = scaled.astype(jnp.bfloat16)
    positive = lax.optimization_barrier(jnp.sum(scaled * target_vec, axis=1))
    weight_pos = -live_mask * jax.nn.sigmoid(-positive)
    negative_vec = jnp.take(target_part, negative_rows.reshape(-1), axis=0).reshape(SPANS, NEG, D).astype(jnp.float32)
    grouped = rounded.reshape(SPANS, CH, D).astype(jnp.float32)
    scores = jnp.einsum('ced,cnd->cen', grouped, negative_vec)
    weight_neg = (live_mask.reshape(SPANS, CH, 1) * jax.nn.sigmoid(scores) * inverse).astype(jnp.bfloat16).astype(jnp.float32)
    pulled = jnp.einsum('cen,cnd->ced', weight_neg, negative_vec).reshape(E_CAP, D)
    pushed = jnp.einsum('cen,ced->cnd', weight_neg, grouped).reshape(SPANS * NEG, D)
    grad_mix = weight_pos[:, None] * target_vec + pulled
    source_grad = jnp.zeros((PROWS_S, D), jnp.float32).at[source_rows].add(relation_vec * grad_mix)
    relation_grad = jnp.zeros((R, D), jnp.float32).at[relation_rows].add(source_vec * grad_mix)
    target_grad = jnp.zeros((PROWS_D, D), jnp.float32).at[target_rows].add(weight_pos[:, None] * scaled)
    target_grad = target_grad.at[negative_rows.reshape(-1)].add(pushed)
    return (source_grad, target_grad, relation_grad)

def reference(src_table, dst_table, rel_diag, src_index, dst_index, rel_index, neg_index, edge_count):

    def visit(carry, bucket):
        grad_source, grad_target, grad_relation = carry
        first = (bucket // N_DST).astype(jnp.int32)
        second = (bucket % N_DST).astype(jnp.int32)
        source_start = (first * PROWS_S).astype(jnp.int32)
        target_start = (second * PROWS_D).astype(jnp.int32)
        source_part = lax.dynamic_slice_in_dim(src_table, source_start, PROWS_S, 0)
        target_part = lax.dynamic_slice_in_dim(dst_table, target_start, PROWS_D, 0)
        source_grad, target_grad, relation_grad = bucket_terms(source_part, target_part, rel_diag, src_index[first, second], dst_index[first, second], rel_index[first, second], neg_index[first, second], edge_count[first, second])
        old_source = lax.dynamic_slice_in_dim(grad_source, source_start, PROWS_S, 0)
        grad_source = lax.dynamic_update_slice_in_dim(grad_source, old_source + source_grad, source_start, 0)
        old_target = lax.dynamic_slice_in_dim(grad_target, target_start, PROWS_D, 0)
        grad_target = lax.dynamic_update_slice_in_dim(grad_target, old_target + target_grad, target_start, 0)
        return ((grad_source, grad_target, grad_relation + relation_grad), None)
    start = (jnp.zeros((N_SRC * PROWS_S, D), jnp.float32), jnp.zeros((N_DST * PROWS_D, D), jnp.float32), jnp.zeros((R, D), jnp.float32))
    result, unused = lax.scan(visit, start, jnp.arange(N_SRC * N_DST, dtype=jnp.int32))
    return (result[0], result[1], result[2])
```

```python
import functools
import math

import jax
import jax.numpy as jnp
from jax import lax
from jax.experimental import pallas as pl
from jax.experimental.pallas import tpu as pltpu
from jax.sharding import PartitionSpec as P

F32, BF16, I32 = jnp.float32, jnp.bfloat16, jnp.int32
NX, NC = 4, 2
SEMS = 160


def dot(a, b):
    return jnp.dot(a, b, preferred_element_type=F32)


def dot_nt(a, b):
    return lax.dot_general(a, b, (((1,), (1,)), ((), ())), preferred_element_type=F32)


def split2(v):
    hi = v.astype(BF16)
    return hi, (v - hi.astype(F32)).astype(BF16)


def kernel(
    nz, nx, ny,
    src_ref, dst_ref, rel_ref, si_ref, di_ref, ri_ref, ni_ref, cnt_ref,
    out_s, out_d, out_r,
    S, T, RF, hot_s, hot_d, hot_r, cold_s, cold_d, cold_r, counts, r_v, q_v, g_v, s_v, t_v, w_v, qb_v, uh_v, ul_v,
    rel_part, rel_sib, rel_xs, rel_xr, rel_zs, rel_zr, rel_ys, rel_yr,
    dst_xs, dst_part, dst_xr, dst_zs, dst_zr,
    src_part, src_sib, src_ys, src_yr,
    send, recv,
):
    a, b = lax.axis_index("src"), lax.axis_index("dst")
    z, x = a // nx, lax.rem(a, nx)
    y, c = b // NC, lax.rem(b, NC)
    o = 1 - c
    rows_s, width = src_ref.shape
    rows_d = dst_ref.shape[0]
    half_s = ny * rows_s
    part_d = nz * rows_d
    n_dst = nx * part_d
    n_rel = rel_ref.shape[0]
    half_r = n_rel // NC
    quart_r = half_r // nx
    edges = si_ref.shape[-1]
    spans, negs = ni_ref.shape[-2], ni_ref.shape[-1]
    per = edges // spans
    inverse = 1.0 / math.sqrt(negs)

    def at_z(k):
        return lax.rem(z + k, nz)

    def at_x(k):
        return lax.rem(x + k, nx)

    def at_y(k):
        return lax.rem(y + k, ny)

    def dev(zz=z, xx=x, yy=y, cc=c):
        return (zz * nx + xx, yy * NC + cc)

    slots = {}
    live_copies = []

    def slot(key):
        return slots.setdefault(key, len(slots))

    def copy(key, src, dst, target):
        k = slot(key)
        return pltpu.make_async_remote_copy(
            src_ref=src, dst_ref=dst, send_sem=send.at[k], recv_sem=recv.at[k],
            device_id=target, device_id_type=pl.DeviceIdType.MESH,
        )

    def start(key, src, dst, target):
        d = copy(key, src, dst, target)
        d.start()
        live_copies.append(d)

    def arrived(key, dst):
        copy(key, dst, dst, dev(cc=o)).wait_recv()

    barrier = pltpu.get_barrier_semaphore()
    peers = [dev(cc=o)]
    peers += [dev(zz=at_z(k)) for k in range(1, nz)]
    peers += [dev(yy=at_y(k)) for k in range(1, ny)]
    peers += [dev(xx=at_x(k)) for k in range(1, nx)]
    for p in peers:
        pl.semaphore_signal(barrier, inc=1, device_id=p, device_id_type=pl.DeviceIdType.MESH)
    S[c, y] = src_ref[...]
    T[x, z] = dst_ref[...]
    pl.semaphore_wait(barrier, len(peers))

    for k in range(1, nz):
        start(("tz", k), dst_ref, T.at[x, z], dev(zz=at_z(k)))
    for k in range(1, ny):
        start(("sy", k), src_ref, S.at[c, y], dev(yy=at_y(k)))
    for e in range(1, nx):
        start(("tx", e, 0), dst_ref, T.at[x, z], dev(xx=at_x(e)))
    start(("sc", 0), src_ref, S.at[c, y], dev(cc=o))

    lx, ls = nx.bit_length() - 1, rows_s.bit_length() - 1

    def order_d(j):
        owner = (j * ((1 << 16) // rows_d + 1)) >> 16
        return j + ((owner & (nx - 1)) * nz + (owner >> lx) - owner) * rows_d

    si = si_ref[...]
    owner = si >> ls
    si = (si & (rows_s - 1)) + (owner & 1) * half_s + (owner >> 1) * rows_s
    di = order_d(di_ref[...])
    ri = ri_ref[...]
    number = lax.broadcasted_iota(I32, (1, edges), 1)
    live_row = jnp.where(number < cnt_ref[...], 1.0, 0.0).astype(F32)
    columns = jnp.concatenate(
        [si.astype(F32), di.astype(F32), ri.astype(F32), live_row, jnp.zeros((4, edges), F32)], axis=0
    ).T
    si_c, di_c, ri_c = (columns[:, k : k + 1].astype(I32) for k in range(3))
    live_col = columns[:, 3:4]

    def hot(index, shape, dim):
        return jnp.where(index == lax.broadcasted_iota(I32, shape, dim), 1.0, 0.0).astype(BF16)

    def forward_z(k):
        zz = at_z(nz - k)
        arrived(("tz", k), T.at[x, zz])
        for e in range(1, nx):
            start(("tx", e, k), T.at[x, zz], T.at[x, zz], dev(xx=at_x(e)))

    def forward_y(k):
        yy = at_y(ny - k)
        arrived(("sy", k), S.at[c, yy])
        start(("sc", k), S.at[c, yy], S.at[c, yy], dev(cc=o))

    hot_r[...] = hot(ri_c, (edges, n_rel), 1)
    hot_s[...] = hot(si_c, (edges, NC * half_s), 1)
    for k in range(1, nz):
        forward_z(k)
    for k in range(1, ny):
        forward_y(k)
    hot_d[...] = hot(di_c, (edges, n_dst), 1)

    rel = rel_ref[...]
    r1, r2 = split2(rel)
    r3 = (rel - r1.astype(F32) - r2.astype(F32)).astype(BF16)
    hr = hot_r[...]
    r_v[...] = dot(hr, r1) + dot(hr, r2) + dot(hr, r3)
    ones = jnp.ones((negs, 128), BF16)
    for m in range(spans):
        nidx = order_d(ni_ref[0, m : m + 1, :])
        counts[m] = dot(hot(nidx, (n_dst, negs), 0), ones)
    cold_r[...] = hot(ri, (n_rel, edges), 0)
    cold_s[...] = hot(si, (NC * half_s, edges), 0)
    cold_d[...] = hot(di, (n_dst, edges), 0)

    for k in range(ny):
        arrived(("sc", k), S.at[o, at_y(ny - k)])
    table_s = S[...].reshape(NC * half_s, width)
    s = dot(hot_s[...], table_s)
    s_v[...] = s
    q = s * r_v[...]
    q_v[...] = q
    qb_v[...] = q.astype(BF16)

    for e in range(1, nx):
        for k in range(nz):
            arrived(("tx", e, k), T.at[at_x(nx - e), at_z(nz - k)])
    table_d = T[...].reshape(n_dst, width)
    t = dot(hot_d[...], table_d)
    t_v[...] = t
    p = jnp.sum(q_v[...] * t, axis=1, keepdims=True)
    w = -live_col * jax.nn.sigmoid(-p)
    w_v[...] = jnp.broadcast_to(w, w_v.shape)
    u32 = table_d.astype(F32)
    for m in range(spans):
        u = u32 * counts[m, :, 0:1]
        uh_v[...], ul_v[...] = split2(u)
        span = pl.ds(m * per, per)
        scores = dot_nt(qb_v[span, :], table_d)
        wn = (live_col[m * per : (m + 1) * per] * jax.nn.sigmoid(scores) * inverse).astype(BF16)
        pulled = dot(wn, uh_v[...]) + dot(wn, ul_v[...])
        g_v[span, :] = w[m * per : (m + 1) * per] * t_v[span, :] + pulled

    sg = s_v[...] * g_v[...]
    h, l = split2(sg)
    theirs = cold_r[pl.ds(o * half_r, half_r), :]
    rel_part[0] = dot(theirs, h) + dot(theirs, l)
    start(("rc",), rel_part.at[0], rel_sib, dev(cc=o))
    mine = cold_r[pl.ds(c * half_r, half_r), :]
    rel_part[1] = dot(mine, h) + dot(mine, l)

    wq = w_v[:, 0:1] * q_v[...]
    h, l = split2(wq)
    for e in [*range(nx // 2, 0, -1), *range(nx // 2 + 1, nx), 0]:
        xx = at_x(e)
        part = pl.ds(xx * part_d, part_d)
        cd = cold_d[part, :]
        total = dot(cd, h) + dot(cd, l)
        tab = T[xx].reshape(part_d, width)
        for m in range(spans):
            qb = qb_v[pl.ds(m * per, per), :]
            scores = dot_nt(tab, qb)
            wn = (live_row[:, m * per : (m + 1) * per] * jax.nn.sigmoid(scores) * inverse).astype(BF16)
            total = total + counts[m, part, 0:1] * dot(wn, qb)
        if e == 0:
            dst_part[...] = total
        else:
            dst_xs[e - 1] = total.astype(BF16).reshape(nz, rows_d, width)
            start(("dx", e), dst_xs.at[e - 1], dst_xr.at[e - 1], dev(xx=xx))

    arrived(("rc",), rel_sib)
    rel_part[1] = rel_part[1] + rel_sib[...]
    for e in range(1, nx):
        rel_xs[e - 1] = rel_part[1, pl.ds(at_x(e) * quart_r, quart_r), :].astype(BF16)
        start(("rx", e), rel_xs.at[e - 1], rel_xr.at[e - 1], dev(xx=at_x(e)))

    rg = r_v[...] * g_v[...]
    h, l = split2(rg)
    theirs = cold_s[pl.ds(o * half_s, half_s), :]
    src_part[0] = dot(theirs, h) + dot(theirs, l)
    start(("ec",), src_part.at[0], src_sib, dev(cc=o))
    mine = cold_s[pl.ds(c * half_s, half_s), :]
    src_part[1] = dot(mine, h) + dot(mine, l)

    total = rel_part[1, pl.ds(x * quart_r, quart_r), :]
    for e in range(1, nx):
        arrived(("rx", e), rel_xr.at[e - 1])
        total = total + rel_xr[e - 1].astype(F32)
    rel_zs[...] = total.reshape(rel_zs.shape)
    for k in range(1, nz):
        start(("rz", k), rel_zs.at[at_z(k)], rel_zr.at[k - 1], dev(zz=at_z(k)))

    for e in range(1, nx):
        arrived(("dx", e), dst_xr.at[e - 1])
    total = dst_part[...]
    for e in range(1, nx):
        total = total + dst_xr[e - 1].astype(F32).reshape(part_d, width)
    dst_zs[...] = total.reshape(dst_zs.shape)
    for k in range(1, nz):
        start(("dz", k), dst_zs.at[at_z(k)], dst_zr.at[k - 1], dev(zz=at_z(k)))

    arrived(("ec",), src_sib)
    src_part[1] = src_part[1] + src_sib[...]
    for k in range(1, ny):
        src_ys[k - 1] = src_part[1, pl.ds(at_y(k) * rows_s, rows_s), :].astype(BF16)
        start(("ey", k), src_ys.at[k - 1], src_yr.at[k - 1], dev(yy=at_y(k)))

    total = rel_zs[z]
    for k in range(1, nz):
        arrived(("rz", k), rel_zr.at[k - 1])
        total = total + rel_zr[k - 1]
    rel_ys[...] = total
    for k in range(1, ny):
        start(("ry", k), rel_ys, rel_yr.at[k - 1], dev(yy=at_y(k)))
    for k in range(1, ny):
        arrived(("ry", k), rel_yr.at[k - 1])
    rel_yr[ny - 1] = total
    total = jnp.zeros(total.shape, F32)
    for yy in range(ny):
        k = lax.rem(y - yy + ny, ny)
        total = total + rel_yr[lax.rem(k + ny - 1, ny)]
    RF[c, x, z] = total

    for k in range(1, nz):
        start(("bz", k), RF.at[c, x, z], RF.at[c, x, z], dev(zz=at_z(k)))
    for e in range(1, nx):
        start(("bx", e, 0), RF.at[c, x, z], RF.at[c, x, z], dev(xx=at_x(e)))
    for k in range(1, nz):
        zz = at_z(nz - k)
        arrived(("bz", k), RF.at[c, x, zz])
        for e in range(1, nx):
            start(("bx", e, k), RF.at[c, x, zz], RF.at[c, x, zz], dev(xx=at_x(e)))
    start(("bc", 0), RF.at[c, x], RF.at[c, x], dev(cc=o))

    total = dst_zs[z]
    for k in range(1, nz):
        arrived(("dz", k), dst_zr.at[k - 1])
        total = total + dst_zr[k - 1]
    out_d[...] = total
    total = src_part[1, pl.ds(y * rows_s, rows_s), :]
    for k in range(1, ny):
        arrived(("ey", k), src_yr.at[k - 1])
        total = total + src_yr[k - 1].astype(F32)
    out_s[...] = total

    for e in range(1, nx):
        xx = at_x(nx - e)
        for k in range(nz):
            arrived(("bx", e, k), RF.at[c, xx, at_z(nz - k)])
        start(("bc", e), RF.at[c, xx], RF.at[c, xx], dev(cc=o))
    out_r[pl.ds(c * half_r, half_r), :] = RF[c].reshape(half_r, width)
    for e in range(nx):
        arrived(("bc", e), RF.at[o, at_x(nx - e)])
    out_r[pl.ds(o * half_r, half_r), :] = RF[o].reshape(half_r, width)

    for d in live_copies:
        d.wait_send()
    assert len(slots) <= SEMS


def per_device(
    nz, nx, ny, src_table, dst_table, rel_diag, src_index, dst_index, rel_index, neg_index, edge_count
):
    rows_s, width = src_table.shape
    rows_d = dst_table.shape[0]
    n_rel = rel_diag.shape[0]
    edges = src_index.shape[-1]
    spans = neg_index.shape[2]
    n_src, n_dst = ny * NC * rows_s, nz * nx * rows_d
    half_r = n_rel // NC
    quart_r = half_r // nx
    eighth_r = quart_r // nz

    def v(shape, kind=F32):
        return pltpu.VMEM(shape, kind)

    return pl.pallas_call(
        functools.partial(kernel, nz, nx, ny),
        out_shape=(
            jax.ShapeDtypeStruct((rows_s, width), F32),
            jax.ShapeDtypeStruct((rows_d, width), F32),
            jax.ShapeDtypeStruct((n_rel, width), F32),
        ),
        in_specs=[pl.BlockSpec(memory_space=pltpu.VMEM)] * 8,
        out_specs=[pl.BlockSpec(memory_space=pltpu.VMEM)] * 3,
        scratch_shapes=[
            v((NC, ny, rows_s, width), BF16),
            v((nx, nz, rows_d, width), BF16),
            v((NC, nx, nz, eighth_r, width)),
            v((edges, n_src), BF16),
            v((edges, n_dst), BF16),
            v((edges, n_rel), BF16),
            v((n_src, edges), BF16),
            v((n_dst, edges), BF16),
            v((n_rel, edges), BF16),
            v((spans, n_dst, 128)),
            v((edges, width)),
            v((edges, width)),
            v((edges, width)),
            v((edges, width)),
            v((edges, width)),
            v((edges, 128)),
            v((edges, width), BF16),
            v((n_dst, width), BF16),
            v((n_dst, width), BF16),
            v((2, half_r, width)),
            v((half_r, width)),
            v((nx - 1, quart_r, width), BF16),
            v((nx - 1, quart_r, width), BF16),
            v((nz, eighth_r, width)),
            v((nz - 1, eighth_r, width)),
            v((eighth_r, width)),
            v((ny, eighth_r, width)),
            v((nx - 1, nz, rows_d, width), BF16),
            v((nz * rows_d, width)),
            v((nx - 1, nz, rows_d, width), BF16),
            v((nz, rows_d, width)),
            v((nz - 1, rows_d, width)),
            v((2, ny * rows_s, width)),
            v((ny * rows_s, width)),
            v((ny - 1, rows_s, width), BF16),
            v((ny - 1, rows_s, width), BF16),
            pltpu.SemaphoreType.DMA((SEMS,)),
            pltpu.SemaphoreType.DMA((SEMS,)),
        ],
        compiler_params=pltpu.CompilerParams(
            collective_id=0, has_side_effects=True, vmem_limit_bytes=50 * 1024 * 1024
        ),
    )(
        src_table, dst_table, rel_diag, src_index[0], dst_index[0], rel_index[0], neg_index[0], edge_count
    )


def solution(mesh):
    sizes = dict(mesh.shape)
    return jax.shard_map(
        functools.partial(per_device, sizes["src"] // NX, NX, sizes["dst"] // NC),
        mesh=mesh,
        in_specs=(
            P(("src", "dst"), None),
            P(("dst", "src"), None),
            P(),
            P("src", "dst", None),
            P("src", "dst", None),
            P("src", "dst", None),
            P("src", "dst", None, None),
            P("src", "dst"),
        ),
        out_specs=(P(("src", "dst"), None), P(("dst", "src"), None), P()),
        check_vma=False,
    )
```

```python
import functools
import math

import jax
import jax.numpy as jnp
from jax import lax
from jax.experimental import pallas as pl
from jax.experimental.pallas import tpu as pltpu
from jax.sharding import PartitionSpec as P

F32, BF16, I32 = jnp.float32, jnp.bfloat16, jnp.int32
NX, NC = 4, 2
SEMS = 192


def dot(a, b):
    return jnp.dot(a, b, preferred_element_type=F32)


def dot_nt(a, b):
    return lax.dot_general(a, b, (((1,), (1,)), ((), ())), preferred_element_type=F32)


def split2(v):
    hi = v.astype(BF16)
    return hi, (v - hi.astype(F32)).astype(BF16)


def kernel(
    nz, nx, ny,
    src_hbm, dst_hbm, rel_hbm, si_hbm, di_hbm, ri_hbm, ni_hbm, cnt_ref,
    out_s, out_d, out_r,
    S, T, rel_v, si_ref, di_ref, ri_ref, ni_ref, hot_s, hot_d, hot_r, cold_s, cold_d, cold_r, counts, r_v, q_v, g_v, s_v, t_v, w_v, qb_v, spread,
    rel_part, rel_sib, rel_xs, rel_xr, a_first, a_got, a_mine, a_all, a_end, b_first, b_got, b_mine, b_all, b_end,
    dst_xs, dst_part, dst_xr, dst_zs, dst_zr, dst_zsb, dst_zrb,
    src_part, src_sib, src_ys, src_yr,
    send, recv, here,
):
    a, b = lax.axis_index("src"), lax.axis_index("dst")
    z, x = a // nx, lax.rem(a, nx)
    y, c = b // NC, lax.rem(b, NC)
    o = 1 - c
    rows_s, width = src_hbm.shape
    rows_d = dst_hbm.shape[0]
    half_s = ny * rows_s
    part_d = nz * rows_d
    n_dst = nx * part_d
    n_rel = rel_v.shape[1]
    half_r = n_rel // NC
    quart_r = half_r // nx
    near = sorted({1, nz - 1})
    cut = a_mine.shape[-1]
    assert ny == nz
    by_distance = sorted(range(1, nz), key=lambda k: min(k, nz - k))
    edges = si_ref.shape[-1]
    spans, negs = ni_ref.shape[-2], ni_ref.shape[-1]
    per = edges // spans
    inverse = 1.0 / math.sqrt(negs)

    def at_z(k):
        return lax.rem(z + k, nz)

    def at_x(k):
        return lax.rem(x + k, nx)

    def at_y(k):
        return lax.rem(y + k, ny)

    def dev(zz=z, xx=x, yy=y, cc=c):
        return (zz * nx + xx, yy * NC + cc)

    slots = {}
    live_copies = []

    def slot(key):
        return slots.setdefault(key, len(slots))

    def copy(key, src, dst, target):
        k = slot(key)
        return pltpu.make_async_remote_copy(
            src_ref=src, dst_ref=dst, send_sem=send.at[k], recv_sem=recv.at[k],
            device_id=target, device_id_type=pl.DeviceIdType.MESH,
        )

    def start(key, src, dst, target):
        d = copy(key, src, dst, target)
        d.start()
        live_copies.append(d)

    def arrived(key, dst):
        copy(key, dst, dst, dev(cc=o)).wait_recv()

    loads = [
        pltpu.make_async_copy(f, t, here.at[k])
        for k, (f, t) in enumerate(
            [
                (dst_hbm, T.at[x, z]), (src_hbm, S.at[c, y]), (ri_hbm, ri_ref), (si_hbm, si_ref),
                (di_hbm, di_ref), (rel_hbm, rel_v), (ni_hbm, ni_ref),
            ]
        )
    ]
    for d in loads:
        d.start()

    barrier = pltpu.get_barrier_semaphore()
    peers = [dev(cc=o)]
    peers += [dev(zz=at_z(k)) for k in range(1, nz)]
    peers += [dev(yy=at_y(k)) for k in range(1, ny)]
    peers += [dev(xx=at_x(k)) for k in range(1, nx)]
    for p in peers:
        pl.semaphore_signal(barrier, inc=1, device_id=p, device_id_type=pl.DeviceIdType.MESH)
    loads[0].wait()
    loads[1].wait()
    pl.semaphore_wait(barrier, len(peers))

    for e in range(1, nx):
        start(("tx", e, 0), T.at[x, z], T.at[x, z], dev(xx=at_x(e)))
    for k in by_distance:
        start(("tz", k), T.at[x, z], T.at[x, z], dev(zz=at_z(k)))
    for k in range(1, ny):
        start(("sy", k), S.at[c, y], S.at[c, y], dev(yy=at_y(k)))
    start(("sc", 0), S.at[c, y], S.at[c, y], dev(cc=o))

    for d in loads[2:]:
        d.wait()
    lx, ls = nx.bit_length() - 1, rows_s.bit_length() - 1

    def order_d(j):
        owner = (j * ((1 << 16) // rows_d + 1)) >> 16
        return j + ((owner & (nx - 1)) * nz + (owner >> lx) - owner) * rows_d

    si = si_ref[...]
    owner = si >> ls
    si = (si & (rows_s - 1)) + (owner & 1) * half_s + (owner >> 1) * rows_s
    di = order_d(di_ref[...])
    ri = ri_ref[...]
    number = lax.broadcasted_iota(I32, (1, edges), 1)
    live_row = jnp.where(number < cnt_ref[...], 1.0, 0.0).astype(F32)
    columns = jnp.concatenate(
        [si.astype(F32), di.astype(F32), ri.astype(F32), live_row, jnp.zeros((4, edges), F32)], axis=0
    ).T
    si_c, di_c, ri_c = (columns[:, k : k + 1].astype(I32) for k in range(3))
    live_col = columns[:, 3:4]

    def hot(index, shape, dim):
        return jnp.where(index == lax.broadcasted_iota(I32, shape, dim), 1.0, 0.0).astype(BF16)

    def forward_z(k):
        zz = at_z(nz - k)
        arrived(("tz", k), T.at[x, zz])
        for e in range(1, nx):
            start(("tx", e, k), T.at[x, zz], T.at[x, zz], dev(xx=at_x(e)))

    def forward_x(e):
        xx = at_x(nx - e)
        arrived(("tx", e, 0), T.at[xx, z])
        for k in near:
            start(("tx", e, k), T.at[xx, z], T.at[xx, z], dev(zz=at_z(k)))

    def forward_y(k):
        yy = at_y(ny - k)
        arrived(("sy", k), S.at[c, yy])
        start(("sc", k), S.at[c, yy], S.at[c, yy], dev(cc=o))

    hot_r[...] = hot(ri_c, (edges, n_rel), 1)
    hot_s[...] = hot(si_c, (edges, NC * half_s), 1)
    forward_x(1)
    forward_x(nx - 1) if nx > 2 else None
    far = [k for k in by_distance if k not in near]
    for k in far[:2]:
        forward_z(k)
    for e in range(2, nx - 1):
        forward_x(e)
    for k in far[2:]:
        forward_z(k)
    for k in range(1, ny):
        forward_y(k)
    for e in range(nx):
        hot_d[e] = hot(di_c - at_x(nx - e) * part_d, (edges, part_d), 1)

    rel = rel_v[...]
    r1, r2 = split2(rel)
    r3 = (rel - r1.astype(F32) - r2.astype(F32)).astype(BF16)
    hr = hot_r[...]
    r_v[...] = dot_nt(hr, r1) + dot_nt(hr, r2) + dot_nt(hr, r3)
    ones = jnp.ones((negs, 128), BF16)
    for m in range(spans):
        nidx = order_d(ni_ref[0, m : m + 1, :])
        counts[m] = dot(hot(nidx, (n_dst, negs), 0), ones)
    cold_r[...] = hot(ri, (n_rel, edges), 0)
    cold_s[...] = hot(si, (NC * half_s, edges), 0)
    cold_d[...] = hot(di, (n_dst, edges), 0)

    for k in range(ny):
        arrived(("sc", k), S.at[o, at_y(ny - k)])
    table_s = S[...].reshape(NC * half_s, width)
    s = dot(hot_s[...], table_s)
    s_v[...] = s
    q = s * r_v[...]
    q_v[...] = q
    qb_v[...] = q.astype(BF16)

    def weights(live, scores):
        return (live * jax.nn.sigmoid(scores) * inverse).astype(BF16)

    def spread_terms(xx):
        part = pl.ds(xx * part_d, part_d)
        tab = T[xx].reshape(part_d, width)
        total = jnp.zeros((part_d, width), F32)
        for m in range(spans):
            qb = qb_v[pl.ds(m * per, per), :]
            wn = weights(live_row[:, m * per : (m + 1) * per], dot_nt(tab, qb))
            total = total + counts[m, part, 0:1] * dot(wn, qb)
        spread[xx] = total

    arrivals = [0, *sorted(range(1, nx), key=lambda e: min(e, nx - e))]
    for n, e in enumerate(arrivals):
        xx = at_x(nx - e)
        if e == 0:
            for k in near:
                arrived(("tz", k), T.at[x, at_z(nz - k)])
        else:
            for k in range(1, nz):
                arrived(("tx", e, k), T.at[xx, at_z(nz - k)])
        tab = T[xx].reshape(part_d, width)
        t = dot(hot_d[e], tab)
        t_v[...] = t if n == 0 else t_v[...] + t
        tab_f = tab.astype(F32)
        for m in range(spans):
            span = pl.ds(m * per, per)
            uh, ul = split2(tab_f * counts[m, pl.ds(xx * part_d, part_d), 0:1])
            wn = weights(live_col[m * per : (m + 1) * per], dot_nt(qb_v[span, :], tab))
            pulled = dot(wn, uh) + dot(wn, ul)
            g_v[span, :] = pulled if n == 0 else g_v[span, :] + pulled
        if n < nx - 1:
            spread_terms(xx)
    p = jnp.sum(q_v[...] * t_v[...], axis=1, keepdims=True)
    w = -live_col * jax.nn.sigmoid(-p)
    w_v[...] = jnp.broadcast_to(w, w_v.shape)
    g_v[...] = w * t_v[...] + g_v[...]

    sg = s_v[...] * g_v[...]
    h, l = split2(sg)
    theirs = cold_r[pl.ds(o * half_r, half_r), :]
    rel_part[0] = dot(theirs, h) + dot(theirs, l)
    order_x = [*range(nx // 2, 0, -1), *range(nx // 2 + 1, nx)]

    def quarter(e):
        return pl.ds(at_x(e) * quart_r, quart_r)

    for e in [*order_x, 0]:
        start(("rc", e), rel_part.at[0, quarter(e)], rel_sib.at[quarter(e)], dev(cc=o))
    mine = cold_r[pl.ds(c * half_r, half_r), :]
    rel_part[1] = dot(mine, h) + dot(mine, l)

    for e in order_x:
        arrived(("rc", e), rel_sib.at[quarter(e)])
        rel_xs[e - 1] = (rel_part[1, quarter(e), :] + rel_sib[quarter(e), :]).astype(BF16)
        start(("rx", e), rel_xs.at[e - 1], rel_xr.at[e - 1], dev(xx=at_x(e)))

    wh, wl = split2(w_v[:, 0:1] * q_v[...])

    def target_terms(e):
        xx = at_x(e)
        cd = cold_d[pl.ds(xx * part_d, part_d), :]
        total = dot(cd, wh) + dot(cd, wl) + spread[xx]
        if e == 0:
            dst_part[...] = total
        else:
            dst_xs[e - 1] = total.astype(BF16).reshape(nz, rows_d, width)
            start(("dx", e), dst_xs.at[e - 1], dst_xr.at[e - 1], dev(xx=xx))

    for e in range(1, nx):
        if e == nx // 2:
            spread_terms(at_x(nx - arrivals[-1]))
        target_terms(e)

    sh, sl = split2(r_v[...] * g_v[...])
    theirs = cold_s[pl.ds(o * half_s, half_s), :]
    src_part[0] = dot(theirs, sh) + dot(theirs, sl)
    start(("ec",), src_part.at[0], src_sib, dev(cc=o))

    arrived(("rc", 0), rel_sib.at[quarter(0)])
    total = rel_part[1, quarter(0), :] + rel_sib[quarter(0), :]
    for e in range(1, nx):
        arrived(("rx", e), rel_xr.at[e - 1])
        total = total + rel_xr[e - 1].astype(F32)
    a_first[...] = total[:, :cut].reshape(a_first.shape)
    b_first[...] = total[:, cut:].reshape(b_first.shape)
    for k in range(1, ny):
        start(("ay", k), a_first.at[at_y(k)], a_got.at[k - 1], dev(yy=at_y(k)))
        start(("bz", k), b_first.at[at_z(k)], b_got.at[k - 1], dev(zz=at_z(k)))

    mine = cold_s[pl.ds(c * half_s, half_s), :]
    src_part[1] = dot(mine, sh) + dot(mine, sl)
    arrived(("ec",), src_sib)
    src_part[1] = src_part[1] + src_sib[...]
    for k in range(1, ny):
        src_ys[k - 1] = src_part[1, pl.ds(at_y(k) * rows_s, rows_s), :].astype(BF16)
        start(("ey", k), src_ys.at[k - 1], src_yr.at[k - 1], dev(yy=at_y(k)))
    target_terms(0)

    ta, tb = a_first[y], b_first[z]
    for k in range(1, ny):
        arrived(("ay", k), a_got.at[k - 1])
        ta = ta + a_got[k - 1]
    a_mine[...] = ta
    for k in range(1, nz):
        start(("az", k), a_mine, a_all.at[k - 1], dev(zz=at_z(k)))
    for k in range(1, nz):
        arrived(("bz", k), b_got.at[k - 1])
        tb = tb + b_got[k - 1]
    b_mine[...] = tb
    for k in range(1, ny):
        start(("by", k), b_mine, b_all.at[k - 1], dev(yy=at_y(k)))
    a_all[nz - 1] = ta
    b_all[ny - 1] = tb

    for e in range(1, nx):
        arrived(("dx", e), dst_xr.at[e - 1])
    total = dst_part[...]
    for e in range(1, nx):
        total = total + dst_xr[e - 1].astype(F32).reshape(part_d, width)
    dst_zs[...] = total.reshape(dst_zs.shape)
    dst_zsb[...] = dst_zs[...].astype(BF16)

    for k in range(1, nz):
        arrived(("az", k), a_all.at[k - 1])
    total = jnp.zeros(a_mine.shape, F32)
    for zz in range(nz):
        total = total + a_all[lax.rem(z - zz + 2 * nz - 1, nz)]
    a_end[c, x, y] = total
    for k in range(1, ny):
        arrived(("by", k), b_all.at[k - 1])
    total = jnp.zeros(b_mine.shape, F32)
    for yy in range(ny):
        total = total + b_all[lax.rem(y - yy + 2 * ny - 1, ny)]
    b_end[c, x, z] = total

    def along_y(k):
        return dev(yy=at_y(k))

    def along_z(k):
        return dev(zz=at_z(k))

    routes = [("A", a_end, at_y, along_y), ("B", b_end, at_z, along_z)]
    for e in range(1, nx):
        for name, end, at, along in routes:
            start((name + "x", e, 0), end.at[c, x, at(0)], end.at[c, x, at(0)], dev(xx=at_x(e)))
    for k in by_distance:
        for name, end, at, along in routes:
            start((name, k), end.at[c, x, at(0)], end.at[c, x, at(0)], along(k))

    def distant(k):
        return 8 * min(k, nz - k) >= 3 * nz

    for k in by_distance[::-1]:
        if distant(k):
            start(("dz", k), dst_zsb.at[at_z(k)], dst_zrb.at[k - 1], dev(zz=at_z(k)))
        else:
            start(("dz", k), dst_zs.at[at_z(k)], dst_zr.at[k - 1], dev(zz=at_z(k)))

    def back_x(e):
        for name, end, at, along in routes:
            block = end.at[c, at_x(nx - e), at(0)]
            arrived((name + "x", e, 0), block)
            for k in near:
                start((name + "x", e, k), block, block, along(k))

    def back_line(k):
        for name, end, at, along in routes:
            block = end.at[c, x, at(nz - k)]
            arrived((name, k), block)
            if k not in near:
                for e in range(1, nx):
                    start((name + "x", e, k), block, block, dev(xx=at_x(e)))

    back_x(1)
    back_x(nx - 1) if nx > 2 else None
    for k in far[:2]:
        back_line(k)
    for e in range(2, nx - 1):
        back_x(e)
    for k in [*far[2:], *near]:
        back_line(k)
    for name, end, at, along in routes:
        start((name + "c", 0), end.at[c, x], end.at[c, x], dev(cc=o))

    for e in range(1, nx):
        xx = at_x(nx - e)
        for name, end, at, along in routes:
            for k in range(1, nz):
                arrived((name + "x", e, k), end.at[c, xx, at(nz - k)])
            start((name + "c", e), end.at[c, xx], end.at[c, xx], dev(cc=o))

    def turn(half):
        lanes = pl.ds(pl.multiple_of(half * half_r, half_r), half_r)
        out_r[0:cut, lanes] = a_end[half].reshape(half_r, cut).T
        out_r[cut:, lanes] = b_end[half].reshape(half_r, width - cut).T

    turn(c)

    total = dst_zs[z]
    for k in range(1, nz):
        if distant(k):
            arrived(("dz", k), dst_zrb.at[k - 1])
            total = total + dst_zrb[k - 1].astype(F32)
        else:
            arrived(("dz", k), dst_zr.at[k - 1])
            total = total + dst_zr[k - 1]
    out_d[...] = total
    total = src_part[1, pl.ds(y * rows_s, rows_s), :]
    for k in range(1, ny):
        arrived(("ey", k), src_yr.at[k - 1])
        total = total + src_yr[k - 1].astype(F32)
    out_s[...] = total

    for e in range(nx):
        for name, end, at, along in routes:
            arrived((name + "c", e), end.at[o, at_x(nx - e)])
    turn(o)
    for d in live_copies:
        d.wait_send()
    assert len(slots) <= SEMS


def per_device(
    nz, nx, ny, src_table, dst_table, rel_diag, src_index, dst_index, rel_index, neg_index, edge_count
):
    rows_s, width = src_table.shape
    rows_d = dst_table.shape[0]
    n_rel = rel_diag.shape[0]
    rel_turned = rel_diag.T
    edges = src_index.shape[-1]
    spans, negs = neg_index.shape[2:]
    n_src, n_dst = ny * NC * rows_s, nz * nx * rows_d
    half_r = n_rel // NC
    quart_r = half_r // nx
    eighth_r = quart_r // ny
    cut = 256

    def v(shape, kind=F32):
        return pltpu.VMEM(shape, kind)

    grads = pl.pallas_call(
        functools.partial(kernel, nz, nx, ny),
        out_shape=(
            pltpu.VMEM((rows_s, width), F32),
            pltpu.VMEM((rows_d, width), F32),
            pltpu.VMEM((width, n_rel), F32),
        ),
        in_specs=[pl.BlockSpec(memory_space=pltpu.HBM)] * 7 + [pl.BlockSpec(memory_space=pltpu.VMEM)],
        out_specs=[pl.BlockSpec(memory_space=pltpu.VMEM)] * 3,
        scratch_shapes=[
            v((NC, ny, rows_s, width), BF16),
            v((nx, nz, rows_d, width), BF16),
            v((width, n_rel)),
            v((1, edges), I32),
            v((1, edges), I32),
            v((1, edges), I32),
            v((1, spans, negs), I32),
            v((edges, n_src), BF16),
            v((nx, edges, nz * rows_d), BF16),
            v((edges, n_rel), BF16),
            v((n_src, edges), BF16),
            v((n_dst, edges), BF16),
            v((n_rel, edges), BF16),
            v((spans, n_dst, 128)),
            v((edges, width)),
            v((edges, width)),
            v((edges, width)),
            v((edges, width)),
            v((edges, width)),
            v((edges, 128)),
            v((edges, width), BF16),
            v((nx, nz * rows_d, width)),
            v((2, half_r, width)),
            v((half_r, width)),
            v((nx - 1, quart_r, width), BF16),
            v((nx - 1, quart_r, width), BF16),
            *(
                v((*lead, eighth_r, wide))
                for wide in (cut, width - cut)
                for lead in ((ny,), (ny - 1,), (), (nz,), (NC, nx, ny))
            ),
            v((nx - 1, nz, rows_d, width), BF16),
            v((nz * rows_d, width)),
            v((nx - 1, nz, rows_d, width), BF16),
            v((nz, rows_d, width)),
            v((nz - 1, rows_d, width)),
            v((nz, rows_d, width), BF16),
            v((nz - 1, rows_d, width), BF16),
            v((2, ny * rows_s, width)),
            v((ny * rows_s, width)),
            v((ny - 1, rows_s, width), BF16),
            v((ny - 1, rows_s, width), BF16),
            pltpu.SemaphoreType.DMA((SEMS,)),
            pltpu.SemaphoreType.DMA((SEMS,)),
            pltpu.SemaphoreType.DMA((7,)),
        ],
        compiler_params=pltpu.CompilerParams(
            collective_id=0, has_side_effects=True, vmem_limit_bytes=50 * 1024 * 1024
        ),
    )(
        *(
            pltpu.with_memory_space_constraint(t, pltpu.HBM)
            for t in (src_table, dst_table, rel_turned, src_index[0], dst_index[0], rel_index[0], neg_index[0])
        ),
        edge_count,
    )
    return grads[0], grads[1], grads[2].T


def solution(mesh):
    sizes = dict(mesh.shape)
    return jax.shard_map(
        functools.partial(per_device, sizes["src"] // NX, NX, sizes["dst"] // NC),
        mesh=mesh,
        in_specs=(
            P(("src", "dst"), None),
            P(("dst", "src"), None),
            P(),
            P("src", "dst", None),
            P("src", "dst", None),
            P("src", "dst", None),
            P("src", "dst", None, None),
            P("src", "dst"),
        ),
        out_specs=(P(("src", "dst"), None), P(("dst", "src"), None), P()),
        check_vma=False,
    )
```

```python
import functools
import math

import jax
import jax.numpy as jnp
from jax import lax
from jax.experimental import pallas as pl
from jax.experimental.pallas import tpu as pltpu
from jax.sharding import PartitionSpec as P

F32, BF16, I32 = jnp.float32, jnp.bfloat16, jnp.int32
NX, NC = 4, 2
SEMS = 192


def dot(a, b):
    return jnp.dot(a, b, preferred_element_type=F32)


def dot_nt(a, b):
    return lax.dot_general(a, b, (((1,), (1,)), ((), ())), preferred_element_type=F32)


def split2(v):
    hi = v.astype(BF16)
    return hi, (v - hi.astype(F32)).astype(BF16)


def kernel(
    nz, nx, ny,
    src_hbm, dst_hbm, rel_hbm, si_hbm, di_hbm, ri_hbm, ni_hbm, cnt_ref,
    out_s, out_d, out_r,
    S, T, rel_v, si_ref, di_ref, ri_ref, ni_ref, hot_s, hot_d, hot_r, cold_s, cold_d, cold_r, counts, r_v, q_v, g_v, s_v, t_v, w_v, qb_v, spread,
    rel_part, rel_sib, rel_xs, rel_xr, a_first, a_got, a_mine, a_all, a_end, b_first, b_got, b_mine, b_all, b_end,
    dst_xs, dst_part, dst_xr, dst_zs, dst_zr, dst_zsb, dst_zrb,
    src_part, src_sib, src_ys, src_yr,
    send, recv, here,
):
    a, b = lax.axis_index("src"), lax.axis_index("dst")
    z, x = a // nx, lax.rem(a, nx)
    y, c = b // NC, lax.rem(b, NC)
    o = 1 - c
    rows_s, width = src_hbm.shape
    rows_d = dst_hbm.shape[0]
    half_s = ny * rows_s
    part_d = nz * rows_d
    n_dst = nx * part_d
    n_rel = rel_v.shape[1]
    half_r = n_rel // NC
    quart_r = half_r // nx
    near = sorted({1, nz - 1})
    cut = a_mine.shape[-1]
    assert ny == nz
    by_distance = sorted(range(1, nz), key=lambda k: min(k, nz - k))
    edges = si_ref.shape[-1]
    spans, negs = ni_ref.shape[-2], ni_ref.shape[-1]
    per = edges // spans
    inverse = 1.0 / math.sqrt(negs)

    def at_z(k):
        return lax.rem(z + k, nz)

    def at_x(k):
        return lax.rem(x + k, nx)

    def at_y(k):
        return lax.rem(y + k, ny)

    def dev(zz=z, xx=x, yy=y, cc=c):
        return (zz * nx + xx, yy * NC + cc)

    slots = {}
    live_copies = []

    def slot(key):
        return slots.setdefault(key, len(slots))

    def copy(key, src, dst, target):
        k = slot(key)
        return pltpu.make_async_remote_copy(
            src_ref=src, dst_ref=dst, send_sem=send.at[k], recv_sem=recv.at[k],
            device_id=target, device_id_type=pl.DeviceIdType.MESH,
        )

    def start(key, src, dst, target):
        d = copy(key, src, dst, target)
        d.start()
        live_copies.append(d)

    def arrived(key, dst):
        copy(key, dst, dst, dev(cc=o)).wait_recv()

    loads = [
        pltpu.make_async_copy(f, t, here.at[k])
        for k, (f, t) in enumerate(
            [
                (dst_hbm, T.at[x, z]), (src_hbm, S.at[c, y]), (ri_hbm, ri_ref), (si_hbm, si_ref),
                (di_hbm, di_ref), (rel_hbm, rel_v), (ni_hbm, ni_ref),
            ]
        )
    ]
    for d in loads:
        d.start()

    barrier = pltpu.get_barrier_semaphore()
    peers = [dev(cc=o)]
    peers += [dev(zz=at_z(k)) for k in range(1, nz)]
    peers += [dev(yy=at_y(k)) for k in range(1, ny)]
    peers += [dev(xx=at_x(k)) for k in range(1, nx)]
    for p in peers:
        pl.semaphore_signal(barrier, inc=1, device_id=p, device_id_type=pl.DeviceIdType.MESH)
    loads[0].wait()
    loads[1].wait()
    pl.semaphore_wait(barrier, len(peers))

    for e in range(1, nx):
        start(("tx", e, 0), T.at[x, z], T.at[x, z], dev(xx=at_x(e)))
    far = [k for k in by_distance if k not in near]
    for k in [*far, *near]:
        start(("tz", k), T.at[x, z], T.at[x, z], dev(zz=at_z(k)))
    for k in range(1, ny):
        start(("sy", k), S.at[c, y], S.at[c, y], dev(yy=at_y(k)))
    start(("sc", 0), S.at[c, y], S.at[c, y], dev(cc=o))

    for d in loads[2:]:
        d.wait()
    lx, ls = nx.bit_length() - 1, rows_s.bit_length() - 1

    def order_d(j):
        owner = (j * ((1 << 16) // rows_d + 1)) >> 16
        return j + ((owner & (nx - 1)) * nz + (owner >> lx) - owner) * rows_d

    si = si_ref[...]
    owner = si >> ls
    si = (si & (rows_s - 1)) + (owner & 1) * half_s + (owner >> 1) * rows_s
    di = order_d(di_ref[...])
    ri = ri_ref[...]
    number = lax.broadcasted_iota(I32, (1, edges), 1)
    live_row = jnp.where(number < cnt_ref[...], 1.0, 0.0).astype(F32)
    columns = jnp.concatenate(
        [si.astype(F32), di.astype(F32), ri.astype(F32), live_row, jnp.zeros((4, edges), F32)], axis=0
    ).T
    si_c, di_c, ri_c = (columns[:, k : k + 1].astype(I32) for k in range(3))
    live_col = columns[:, 3:4]

    def hot(index, shape, dim):
        return jnp.where(index == lax.broadcasted_iota(I32, shape, dim), 1.0, 0.0).astype(BF16)

    def forward_z(k):
        zz = at_z(nz - k)
        arrived(("tz", k), T.at[x, zz])
        for e in range(1, nx):
            start(("tx", e, k), T.at[x, zz], T.at[x, zz], dev(xx=at_x(e)))

    def forward_x(e):
        xx = at_x(nx - e)
        arrived(("tx", e, 0), T.at[xx, z])
        for k in near:
            start(("tx", e, k), T.at[xx, z], T.at[xx, z], dev(zz=at_z(k)))

    def forward_y(k):
        yy = at_y(ny - k)
        arrived(("sy", k), S.at[c, yy])
        start(("sc", k), S.at[c, yy], S.at[c, yy], dev(cc=o))

    hot_r[...] = hot(ri_c, (edges, n_rel), 1)
    hot_s[...] = hot(si_c, (edges, NC * half_s), 1)
    forward_x(1)
    forward_x(nx - 1) if nx > 2 else None
    for k in far[:2]:
        forward_z(k)
    for e in range(2, nx - 1):
        forward_x(e)
    for k in far[2:]:
        forward_z(k)
    for k in range(1, ny):
        forward_y(k)
    for e in range(nx):
        hot_d[e] = hot(di_c - at_x(nx - e) * part_d, (edges, part_d), 1)

    rel = rel_v[...]
    r1, r2 = split2(rel)
    r3 = (rel - r1.astype(F32) - r2.astype(F32)).astype(BF16)
    hr = hot_r[...]
    r_v[...] = dot_nt(hr, r1) + dot_nt(hr, r2) + dot_nt(hr, r3)
    ones = jnp.ones((negs, 128), BF16)
    for m in range(spans):
        nidx = order_d(ni_ref[0, m : m + 1, :])
        counts[m] = dot(hot(nidx, (n_dst, negs), 0), ones)
    cold_r[...] = hot(ri, (n_rel, edges), 0)
    cold_s[...] = hot(si, (NC * half_s, edges), 0)
    cold_d[...] = hot(di, (n_dst, edges), 0)

    for k in range(ny):
        arrived(("sc", k), S.at[o, at_y(ny - k)])
    table_s = S[...].reshape(NC * half_s, width)
    s = dot(hot_s[...], table_s)
    s_v[...] = s
    q = s * r_v[...]
    q_v[...] = q
    qb_v[...] = q.astype(BF16)

    def weights(live, scores):
        return (live * jax.nn.sigmoid(scores) * inverse).astype(BF16)

    def spread_terms(xx):
        part = pl.ds(xx * part_d, part_d)
        tab = T[xx].reshape(part_d, width)
        total = jnp.zeros((part_d, width), F32)
        for m in range(spans):
            qb = qb_v[pl.ds(m * per, per), :]
            wn = weights(live_row[:, m * per : (m + 1) * per], dot_nt(tab, qb))
            total = total + counts[m, part, 0:1] * dot(wn, qb)
        spread[xx] = total

    arrivals = [0, *sorted(range(1, nx), key=lambda e: min(e, nx - e))]
    for n, e in enumerate(arrivals):
        xx = at_x(nx - e)
        if e == 0:
            for k in near:
                arrived(("tz", k), T.at[x, at_z(nz - k)])
        else:
            for k in range(1, nz):
                arrived(("tx", e, k), T.at[xx, at_z(nz - k)])
        tab = T[xx].reshape(part_d, width)
        t = dot(hot_d[e], tab)
        t_v[...] = t if n == 0 else t_v[...] + t
        tab_f = tab.astype(F32)
        for m in range(spans):
            span = pl.ds(m * per, per)
            uh, ul = split2(tab_f * counts[m, pl.ds(xx * part_d, part_d), 0:1])
            wn = weights(live_col[m * per : (m + 1) * per], dot_nt(qb_v[span, :], tab))
            pulled = dot(wn, uh) + dot(wn, ul)
            g_v[span, :] = pulled if n == 0 else g_v[span, :] + pulled
        if n < nx - 1:
            spread_terms(xx)
    p = jnp.sum(q_v[...] * t_v[...], axis=1, keepdims=True)
    w = -live_col * jax.nn.sigmoid(-p)
    w_v[...] = jnp.broadcast_to(w, w_v.shape)
    g_v[...] = w * t_v[...] + g_v[...]

    sg = s_v[...] * g_v[...]
    h, l = split2(sg)
    theirs = cold_r[pl.ds(o * half_r, half_r), :]
    rel_part[0] = dot(theirs, h) + dot(theirs, l)
    order_x = [*range(nx // 2, 0, -1), *range(nx // 2 + 1, nx)]

    def quarter(e):
        return pl.ds(at_x(e) * quart_r, quart_r)

    for e in [*order_x, 0]:
        start(("rc", e), rel_part.at[0, quarter(e)], rel_sib.at[quarter(e)], dev(cc=o))
    mine = cold_r[pl.ds(c * half_r, half_r), :]
    rel_part[1] = dot(mine, h) + dot(mine, l)

    for e in order_x:
        arrived(("rc", e), rel_sib.at[quarter(e)])
        rel_xs[e - 1] = (rel_part[1, quarter(e), :] + rel_sib[quarter(e), :]).astype(BF16)
        start(("rx", e), rel_xs.at[e - 1], rel_xr.at[e - 1], dev(xx=at_x(e)))

    wh, wl = split2(w_v[:, 0:1] * q_v[...])

    def target_terms(e):
        xx = at_x(e)
        cd = cold_d[pl.ds(xx * part_d, part_d), :]
        total = dot(cd, wh) + dot(cd, wl) + spread[xx]
        if e == 0:
            dst_part[...] = total
        else:
            dst_xs[e - 1] = total.astype(BF16).reshape(nz, rows_d, width)
            start(("dx", e), dst_xs.at[e - 1], dst_xr.at[e - 1], dev(xx=xx))

    for e in range(1, nx):
        if e == nx // 2:
            spread_terms(at_x(nx - arrivals[-1]))
        target_terms(e)

    sh, sl = split2(r_v[...] * g_v[...])
    theirs = cold_s[pl.ds(o * half_s, half_s), :]
    src_part[0] = dot(theirs, sh) + dot(theirs, sl)
    start(("ec",), src_part.at[0], src_sib, dev(cc=o))

    arrived(("rc", 0), rel_sib.at[quarter(0)])
    total = rel_part[1, quarter(0), :] + rel_sib[quarter(0), :]
    for e in range(1, nx):
        arrived(("rx", e), rel_xr.at[e - 1])
        total = total + rel_xr[e - 1].astype(F32)
    a_first[...] = total[:, :cut].reshape(a_first.shape)
    b_first[...] = total[:, cut:].reshape(b_first.shape)
    for k in range(1, ny):
        start(("ay", k), a_first.at[at_y(k)], a_got.at[k - 1], dev(yy=at_y(k)))
        start(("bz", k), b_first.at[at_z(k)], b_got.at[k - 1], dev(zz=at_z(k)))

    mine = cold_s[pl.ds(c * half_s, half_s), :]
    src_part[1] = dot(mine, sh) + dot(mine, sl)
    arrived(("ec",), src_sib)
    src_part[1] = src_part[1] + src_sib[...]
    for k in range(1, ny):
        src_ys[k - 1] = src_part[1, pl.ds(at_y(k) * rows_s, rows_s), :].astype(BF16)
    target_terms(0)

    ta, tb = a_first[y], b_first[z]
    for k in range(1, ny):
        arrived(("ay", k), a_got.at[k - 1])
        ta = ta + a_got[k - 1]
    a_mine[...] = ta
    for k in range(1, nz):
        start(("az", k), a_mine, a_all.at[k - 1], dev(zz=at_z(k)))
    for k in range(1, nz):
        arrived(("bz", k), b_got.at[k - 1])
        tb = tb + b_got[k - 1]
    b_mine[...] = tb
    for k in range(1, ny):
        start(("by", k), b_mine, b_all.at[k - 1], dev(yy=at_y(k)))
    a_all[nz - 1] = ta
    b_all[ny - 1] = tb

    for k in range(1, ny):
        start(("ey", k), src_ys.at[k - 1], src_yr.at[k - 1], dev(yy=at_y(k)))

    for e in range(1, nx):
        arrived(("dx", e), dst_xr.at[e - 1])
    total = dst_part[...]
    for e in range(1, nx):
        total = total + dst_xr[e - 1].astype(F32).reshape(part_d, width)
    dst_zs[...] = total.reshape(dst_zs.shape)
    dst_zsb[...] = dst_zs[...].astype(BF16)

    def distant(k):
        return 8 * min(k, nz - k) >= 3 * nz

    for k in by_distance[::-1]:
        if distant(k):
            start(("dz", k), dst_zsb.at[at_z(k)], dst_zrb.at[k - 1], dev(zz=at_z(k)))
        else:
            start(("dz", k), dst_zs.at[at_z(k)], dst_zr.at[k - 1], dev(zz=at_z(k)))

    for k in range(1, nz):
        arrived(("az", k), a_all.at[k - 1])
    total = jnp.zeros(a_mine.shape, F32)
    for zz in range(nz):
        total = total + a_all[lax.rem(z - zz + 2 * nz - 1, nz)]
    a_end[c, x, y] = total
    for k in range(1, ny):
        arrived(("by", k), b_all.at[k - 1])
    total = jnp.zeros(b_mine.shape, F32)
    for yy in range(ny):
        total = total + b_all[lax.rem(y - yy + 2 * ny - 1, ny)]
    b_end[c, x, z] = total

    def along_y(k):
        return dev(yy=at_y(k))

    def along_z(k):
        return dev(zz=at_z(k))

    routes = [("A", a_end, at_y, along_y), ("B", b_end, at_z, along_z)]
    def back_own(k):
        for name, end, at, along in routes:
            start((name, k), end.at[c, x, at(0)], end.at[c, x, at(0)], along(k))

    for k in far[::-1]:
        back_own(k)
    for e in range(1, nx):
        for name, end, at, along in routes:
            start((name + "x", e, 0), end.at[c, x, at(0)], end.at[c, x, at(0)], dev(xx=at_x(e)))
    for k in near:
        back_own(k)

    def back_x(e):
        for name, end, at, along in routes:
            block = end.at[c, at_x(nx - e), at(0)]
            arrived((name + "x", e, 0), block)
            for k in near:
                start((name + "x", e, k), block, block, along(k))

    def back_line(k):
        for name, end, at, along in routes:
            block = end.at[c, x, at(nz - k)]
            arrived((name, k), block)
            if k not in near:
                for e in range(1, nx):
                    start((name + "x", e, k), block, block, dev(xx=at_x(e)))

    back_x(1)
    back_x(nx - 1) if nx > 2 else None
    for k in far[:2]:
        back_line(k)
    for e in range(2, nx - 1):
        back_x(e)
    for k in [*far[2:], *near]:
        back_line(k)
    for name, end, at, along in routes:
        start((name + "c", 0), end.at[c, x], end.at[c, x], dev(cc=o))

    for e in range(1, nx):
        xx = at_x(nx - e)
        for name, end, at, along in routes:
            for k in range(1, nz):
                arrived((name + "x", e, k), end.at[c, xx, at(nz - k)])
            start((name + "c", e), end.at[c, xx], end.at[c, xx], dev(cc=o))

    def turn(half):
        lanes = pl.ds(pl.multiple_of(half * half_r, half_r), half_r)
        out_r[0:cut, lanes] = a_end[half].reshape(half_r, cut).T
        out_r[cut:, lanes] = b_end[half].reshape(half_r, width - cut).T

    turn(c)

    total = dst_zs[z]
    for k in range(1, nz):
        if distant(k):
            arrived(("dz", k), dst_zrb.at[k - 1])
            total = total + dst_zrb[k - 1].astype(F32)
        else:
            arrived(("dz", k), dst_zr.at[k - 1])
            total = total + dst_zr[k - 1]
    out_d[...] = total
    total = src_part[1, pl.ds(y * rows_s, rows_s), :]
    for k in range(1, ny):
        arrived(("ey", k), src_yr.at[k - 1])
        total = total + src_yr[k - 1].astype(F32)
    out_s[...] = total

    for e in range(nx):
        for name, end, at, along in routes:
            arrived((name + "c", e), end.at[o, at_x(nx - e)])
    turn(o)
    for d in live_copies:
        d.wait_send()
    assert len(slots) <= SEMS


def per_device(
    nz, nx, ny, src_table, dst_table, rel_diag, src_index, dst_index, rel_index, neg_index, edge_count
):
    rows_s, width = src_table.shape
    rows_d = dst_table.shape[0]
    n_rel = rel_diag.shape[0]
    rel_turned = rel_diag.T
    edges = src_index.shape[-1]
    spans, negs = neg_index.shape[2:]
    n_src, n_dst = ny * NC * rows_s, nz * nx * rows_d
    half_r = n_rel // NC
    quart_r = half_r // nx
    eighth_r = quart_r // ny
    cut = 256

    def v(shape, kind=F32):
        return pltpu.VMEM(shape, kind)

    grads = pl.pallas_call(
        functools.partial(kernel, nz, nx, ny),
        out_shape=(
            pltpu.VMEM((rows_s, width), F32),
            pltpu.VMEM((rows_d, width), F32),
            pltpu.VMEM((width, n_rel), F32),
        ),
        in_specs=[pl.BlockSpec(memory_space=pltpu.HBM)] * 7 + [pl.BlockSpec(memory_space=pltpu.VMEM)],
        out_specs=[pl.BlockSpec(memory_space=pltpu.VMEM)] * 3,
        scratch_shapes=[
            v((NC, ny, rows_s, width), BF16),
            v((nx, nz, rows_d, width), BF16),
            v((width, n_rel)),
            v((1, edges), I32),
            v((1, edges), I32),
            v((1, edges), I32),
            v((1, spans, negs), I32),
            v((edges, n_src), BF16),
            v((nx, edges, nz * rows_d), BF16),
            v((edges, n_rel), BF16),
            v((n_src, edges), BF16),
            v((n_dst, edges), BF16),
            v((n_rel, edges), BF16),
            v((spans, n_dst, 128)),
            v((edges, width)),
            v((edges, width)),
            v((edges, width)),
            v((edges, width)),
            v((edges, width)),
            v((edges, 128)),
            v((edges, width), BF16),
            v((nx, nz * rows_d, width)),
            v((2, half_r, width)),
            v((half_r, width)),
            v((nx - 1, quart_r, width), BF16),
            v((nx - 1, quart_r, width), BF16),
            *(
                v((*lead, eighth_r, wide))
                for wide in (cut, width - cut)
                for lead in ((ny,), (ny - 1,), (), (nz,), (NC, nx, ny))
            ),
            v((nx - 1, nz, rows_d, width), BF16),
            v((nz * rows_d, width)),
            v((nx - 1, nz, rows_d, width), BF16),
            v((nz, rows_d, width)),
            v((nz - 1, rows_d, width)),
            v((nz, rows_d, width), BF16),
            v((nz - 1, rows_d, width), BF16),
            v((2, ny * rows_s, width)),
            v((ny * rows_s, width)),
            v((ny - 1, rows_s, width), BF16),
            v((ny - 1, rows_s, width), BF16),
            pltpu.SemaphoreType.DMA((SEMS,)),
            pltpu.SemaphoreType.DMA((SEMS,)),
            pltpu.SemaphoreType.DMA((7,)),
        ],
        compiler_params=pltpu.CompilerParams(
            collective_id=0, has_side_effects=True, vmem_limit_bytes=50 * 1024 * 1024
        ),
    )(
        *(
            pltpu.with_memory_space_constraint(t, pltpu.HBM)
            for t in (src_table, dst_table, rel_turned, src_index[0], dst_index[0], rel_index[0], neg_index[0])
        ),
        edge_count,
    )
    return grads[0], grads[1], grads[2].T


def solution(mesh):
    sizes = dict(mesh.shape)
    return jax.shard_map(
        functools.partial(per_device, sizes["src"] // NX, NX, sizes["dst"] // NC),
        mesh=mesh,
        in_specs=(
            P(("src", "dst"), None),
            P(("dst", "src"), None),
            P(),
            P("src", "dst", None),
            P("src", "dst", None),
            P("src", "dst", None),
            P("src", "dst", None, None),
            P("src", "dst"),
        ),
        out_specs=(P(("src", "dst"), None), P(("dst", "src"), None), P()),
        check_vma=False,
    )
```

```python
import functools
import math

import jax
import jax.numpy as jnp
from jax import lax
from jax.experimental import pallas as pl
from jax.experimental.pallas import tpu as pltpu
from jax.sharding import PartitionSpec as P

F32, BF16, I32 = jnp.float32, jnp.bfloat16, jnp.int32
NX, NC = 4, 2
SEMS = 192


def dot(a, b):
    return jnp.dot(a, b, preferred_element_type=F32)


def dot_nt(a, b):
    return lax.dot_general(a, b, (((1,), (1,)), ((), ())), preferred_element_type=F32)


def split2(v):
    hi = v.astype(BF16)
    return hi, (v - hi.astype(F32)).astype(BF16)


def kernel(
    nz, nx, ny,
    src_hbm, dst_hbm, rel_hbm, si_hbm, di_hbm, ri_hbm, ni_hbm, cnt_ref,
    out_s, out_d, out_r,
    S, T, rel_v, si_ref, di_ref, ri_ref, ni_ref, hot_s, hot_d, hot_r, cold_s, cold_d, cold_r, counts, r_v, q_v, g_v, s_v, t_v, w_v, qb_v, spread,
    rel_part, rel_sib, rel_xs, rel_xr, a_first, a_got, a_mine, a_all, a_end, b_first, b_got, b_mine, b_all, b_end,
    dst_xs, dst_part, dst_xr, dst_zs, dst_zsb, dst_zrb,
    src_part, src_sib, src_ys, src_yr,
    send, recv, here,
):
    a, b = lax.axis_index("src"), lax.axis_index("dst")
    z, x = a // nx, lax.rem(a, nx)
    y, c = b // NC, lax.rem(b, NC)
    o = 1 - c
    rows_s, width = src_hbm.shape
    rows_d = dst_hbm.shape[0]
    half_s = ny * rows_s
    part_d = nz * rows_d
    n_dst = nx * part_d
    n_rel = rel_v.shape[1]
    half_r = n_rel // NC
    quart_r = half_r // nx
    near = sorted({1, nz - 1})
    cut = a_mine.shape[-1]
    assert ny == nz
    by_distance = sorted(range(1, nz), key=lambda k: min(k, nz - k))
    edges = si_ref.shape[-1]
    spans, negs = ni_ref.shape[-2], ni_ref.shape[-1]
    per = edges // spans
    inverse = 1.0 / math.sqrt(negs)

    def at_z(k):
        return lax.rem(z + k, nz)

    def at_x(k):
        return lax.rem(x + k, nx)

    def at_y(k):
        return lax.rem(y + k, ny)

    def dev(zz=z, xx=x, yy=y, cc=c):
        return (zz * nx + xx, yy * NC + cc)

    slots = {}
    live_copies = []

    def slot(key):
        return slots.setdefault(key, len(slots))

    def copy(key, src, dst, target):
        k = slot(key)
        return pltpu.make_async_remote_copy(
            src_ref=src, dst_ref=dst, send_sem=send.at[k], recv_sem=recv.at[k],
            device_id=target, device_id_type=pl.DeviceIdType.MESH,
        )

    def start(key, src, dst, target):
        d = copy(key, src, dst, target)
        d.start()
        live_copies.append(d)

    def arrived(key, dst):
        copy(key, dst, dst, dev(cc=o)).wait_recv()

    loads = [
        pltpu.make_async_copy(f, t, here.at[k])
        for k, (f, t) in enumerate(
            [
                (dst_hbm, T.at[x, z]), (src_hbm, S.at[c, y]), (ri_hbm, ri_ref), (si_hbm, si_ref),
                (di_hbm, di_ref), (rel_hbm, rel_v), (ni_hbm, ni_ref),
            ]
        )
    ]
    for d in loads:
        d.start()

    barrier = pltpu.get_barrier_semaphore()
    peers = [dev(cc=o)]
    peers += [dev(zz=at_z(k)) for k in range(1, nz)]
    peers += [dev(yy=at_y(k)) for k in range(1, ny)]
    peers += [dev(xx=at_x(k)) for k in range(1, nx)]
    for p in peers:
        pl.semaphore_signal(barrier, inc=1, device_id=p, device_id_type=pl.DeviceIdType.MESH)
    loads[0].wait()
    loads[1].wait()
    pl.semaphore_wait(barrier, len(peers))

    for e in range(1, nx):
        start(("tx", e, 0), T.at[x, z], T.at[x, z], dev(xx=at_x(e)))
    far = [k for k in by_distance if k not in near]
    for k in [*far, *near]:
        start(("tz", k), T.at[x, z], T.at[x, z], dev(zz=at_z(k)))
    for k in range(1, ny):
        start(("sy", k), S.at[c, y], S.at[c, y], dev(yy=at_y(k)))
    start(("sc", 0), S.at[c, y], S.at[c, y], dev(cc=o))

    for d in loads[2:]:
        d.wait()
    lx, ls = nx.bit_length() - 1, rows_s.bit_length() - 1

    def order_d(j):
        owner = (j * ((1 << 16) // rows_d + 1)) >> 16
        return j + ((owner & (nx - 1)) * nz + (owner >> lx) - owner) * rows_d

    si = si_ref[...]
    owner = si >> ls
    si = (si & (rows_s - 1)) + (owner & 1) * half_s + (owner >> 1) * rows_s
    di = order_d(di_ref[...])
    ri = ri_ref[...]
    number = lax.broadcasted_iota(I32, (1, edges), 1)
    live_row = jnp.where(number < cnt_ref[...], 1.0, 0.0).astype(F32)
    columns = jnp.concatenate(
        [si.astype(F32), di.astype(F32), ri.astype(F32), live_row, jnp.zeros((4, edges), F32)], axis=0
    ).T
    si_c, di_c, ri_c = (columns[:, k : k + 1].astype(I32) for k in range(3))
    live_col = columns[:, 3:4]

    def hot(index, shape, dim):
        return jnp.where(index == lax.broadcasted_iota(I32, shape, dim), 1.0, 0.0).astype(BF16)

    def forward_z(k):
        zz = at_z(nz - k)
        arrived(("tz", k), T.at[x, zz])
        for e in range(1, nx):
            start(("tx", e, k), T.at[x, zz], T.at[x, zz], dev(xx=at_x(e)))

    def forward_x(e):
        xx = at_x(nx - e)
        arrived(("tx", e, 0), T.at[xx, z])
        for k in near:
            start(("tx", e, k), T.at[xx, z], T.at[xx, z], dev(zz=at_z(k)))

    def forward_y(k):
        yy = at_y(ny - k)
        arrived(("sy", k), S.at[c, yy])
        start(("sc", k), S.at[c, yy], S.at[c, yy], dev(cc=o))

    hot_r[...] = hot(ri_c, (edges, n_rel), 1)
    hot_s[...] = hot(si_c, (edges, NC * half_s), 1)
    forward_x(1)
    forward_x(nx - 1) if nx > 2 else None
    for k in far[:2]:
        forward_z(k)
    for e in range(2, nx - 1):
        forward_x(e)
    for k in far[2:]:
        forward_z(k)
    for k in range(1, ny):
        forward_y(k)
    for e in range(nx):
        hot_d[e] = hot(di_c - at_x(nx - e) * part_d, (edges, part_d), 1)

    rel = rel_v[...]
    r1, r2 = split2(rel)
    r3 = (rel - r1.astype(F32) - r2.astype(F32)).astype(BF16)
    hr = hot_r[...]
    r_v[...] = dot_nt(hr, r1) + dot_nt(hr, r2) + dot_nt(hr, r3)
    ones = jnp.ones((negs, 128), BF16)
    for m in range(spans):
        nidx = order_d(ni_ref[0, m : m + 1, :])
        counts[m] = dot(hot(nidx, (n_dst, negs), 0), ones)
    cold_r[...] = hot(ri, (n_rel, edges), 0)
    cold_s[...] = hot(si, (NC * half_s, edges), 0)
    cold_d[...] = hot(di, (n_dst, edges), 0)

    for k in range(ny):
        arrived(("sc", k), S.at[o, at_y(ny - k)])
    table_s = S[...].reshape(NC * half_s, width)
    s = dot(hot_s[...], table_s)
    s_v[...] = s
    q = s * r_v[...]
    q_v[...] = q
    qb_v[...] = q.astype(BF16)

    def weights(live, scores):
        return (live * jax.nn.sigmoid(scores) * inverse).astype(BF16)

    def spread_terms(xx):
        part = pl.ds(xx * part_d, part_d)
        tab = T[xx].reshape(part_d, width)
        total = jnp.zeros((part_d, width), F32)
        for m in range(spans):
            qb = qb_v[pl.ds(m * per, per), :]
            wn = weights(live_row[:, m * per : (m + 1) * per], dot_nt(tab, qb))
            total = total + counts[m, part, 0:1] * dot(wn, qb)
        spread[xx] = total

    arrivals = [0, *sorted(range(1, nx), key=lambda e: min(e, nx - e))]
    for n, e in enumerate(arrivals):
        xx = at_x(nx - e)
        if e == 0:
            for k in near:
                arrived(("tz", k), T.at[x, at_z(nz - k)])
        else:
            for k in range(1, nz):
                arrived(("tx", e, k), T.at[xx, at_z(nz - k)])
        tab = T[xx].reshape(part_d, width)
        t = dot(hot_d[e], tab)
        t_v[...] = t if n == 0 else t_v[...] + t
        tab_f = tab.astype(F32)
        for m in range(spans):
            span = pl.ds(m * per, per)
            uh, ul = split2(tab_f * counts[m, pl.ds(xx * part_d, part_d), 0:1])
            wn = weights(live_col[m * per : (m + 1) * per], dot_nt(qb_v[span, :], tab))
            pulled = dot(wn, uh) + dot(wn, ul)
            g_v[span, :] = pulled if n == 0 else g_v[span, :] + pulled
        if n == 0:
            spread_terms(xx)
    p = jnp.sum(q_v[...] * t_v[...], axis=1, keepdims=True)
    w = -live_col * jax.nn.sigmoid(-p)
    w_v[...] = jnp.broadcast_to(w, w_v.shape)
    g_v[...] = w * t_v[...] + g_v[...]

    sg = s_v[...] * g_v[...]
    h, l = split2(sg)
    theirs = cold_r[pl.ds(o * half_r, half_r), :]
    rel_part[0] = dot(theirs, h) + dot(theirs, l)
    order_x = [*range(nx // 2, 0, -1), *range(nx // 2 + 1, nx)]

    def quarter(e):
        return pl.ds(at_x(e) * quart_r, quart_r)

    for e in [*order_x, 0]:
        start(("rc", e), rel_part.at[0, quarter(e)], rel_sib.at[quarter(e)], dev(cc=o))
    mine = cold_r[pl.ds(c * half_r, half_r), :]
    rel_part[1] = dot(mine, h) + dot(mine, l)

    for e in order_x:
        arrived(("rc", e), rel_sib.at[quarter(e)])
        rel_xs[e - 1] = (rel_part[1, quarter(e), :] + rel_sib[quarter(e), :]).astype(BF16)
        start(("rx", e), rel_xs.at[e - 1], rel_xr.at[e - 1], dev(xx=at_x(e)))

    wh, wl = split2(w_v[:, 0:1] * q_v[...])

    def target_terms(e):
        xx = at_x(e)
        cd = cold_d[pl.ds(xx * part_d, part_d), :]
        total = dot(cd, wh) + dot(cd, wl) + spread[xx]
        if e == 0:
            dst_part[...] = total
        else:
            dst_xs[e - 1] = total.astype(BF16).reshape(nz, rows_d, width)
            start(("dx", e), dst_xs.at[e - 1], dst_xr.at[e - 1], dev(xx=xx))

    for e in range(1, nx):
        spread_terms(at_x(e))
        target_terms(e)

    sh, sl = split2(r_v[...] * g_v[...])
    theirs = cold_s[pl.ds(o * half_s, half_s), :]
    src_part[0] = dot(theirs, sh) + dot(theirs, sl)
    start(("ec",), src_part.at[0], src_sib, dev(cc=o))

    arrived(("rc", 0), rel_sib.at[quarter(0)])
    total = rel_part[1, quarter(0), :] + rel_sib[quarter(0), :]
    for e in range(1, nx):
        arrived(("rx", e), rel_xr.at[e - 1])
        total = total + rel_xr[e - 1].astype(F32)
    a_first[...] = total[:, :cut].reshape(a_first.shape)
    b_first[...] = total[:, cut:].reshape(b_first.shape)
    for k in range(1, ny):
        start(("ay", k), a_first.at[at_y(k)], a_got.at[k - 1], dev(yy=at_y(k)))
        start(("bz", k), b_first.at[at_z(k)], b_got.at[k - 1], dev(zz=at_z(k)))

    mine = cold_s[pl.ds(c * half_s, half_s), :]
    src_part[1] = dot(mine, sh) + dot(mine, sl)
    arrived(("ec",), src_sib)
    src_part[1] = src_part[1] + src_sib[...]
    for k in range(1, ny):
        src_ys[k - 1] = src_part[1, pl.ds(at_y(k) * rows_s, rows_s), :].astype(BF16)
    target_terms(0)

    ta, tb = a_first[y], b_first[z]
    for k in range(1, ny):
        arrived(("ay", k), a_got.at[k - 1])
        ta = ta + a_got[k - 1]
    a_mine[...] = ta
    for k in range(1, nz):
        start(("az", k), a_mine, a_all.at[k - 1], dev(zz=at_z(k)))
    for k in range(1, nz):
        arrived(("bz", k), b_got.at[k - 1])
        tb = tb + b_got[k - 1]
    b_mine[...] = tb
    for k in range(1, ny):
        start(("by", k), b_mine, b_all.at[k - 1], dev(yy=at_y(k)))
    a_all[nz - 1] = ta
    b_all[ny - 1] = tb

    for k in range(1, ny):
        start(("ey", k), src_ys.at[k - 1], src_yr.at[k - 1], dev(yy=at_y(k)))

    for k in range(1, nz):
        arrived(("az", k), a_all.at[k - 1])
    total = jnp.zeros(a_mine.shape, F32)
    for zz in range(nz):
        total = total + a_all[lax.rem(z - zz + 2 * nz - 1, nz)]
    a_end[c, x, y] = total
    for k in range(1, ny):
        arrived(("by", k), b_all.at[k - 1])
    total = jnp.zeros(b_mine.shape, F32)
    for yy in range(ny):
        total = total + b_all[lax.rem(y - yy + 2 * ny - 1, ny)]
    b_end[c, x, z] = total

    def along_y(k):
        return dev(yy=at_y(k))

    def along_z(k):
        return dev(zz=at_z(k))

    routes = [("A", a_end, at_y, along_y), ("B", b_end, at_z, along_z)]
    def back_own(k):
        for name, end, at, along in routes:
            start((name, k), end.at[c, x, at(0)], end.at[c, x, at(0)], along(k))

    for k in far[::-1]:
        back_own(k)
    for e in range(1, nx):
        for name, end, at, along in routes:
            start((name + "x", e, 0), end.at[c, x, at(0)], end.at[c, x, at(0)], dev(xx=at_x(e)))
    for k in near:
        back_own(k)

    for e in range(1, nx):
        arrived(("dx", e), dst_xr.at[e - 1])
    total = dst_part[...]
    for e in range(1, nx):
        total = total + dst_xr[e - 1].astype(F32).reshape(part_d, width)
    dst_zs[...] = total.reshape(dst_zs.shape)
    dst_zsb[...] = dst_zs[...].astype(BF16)

    for k in by_distance[::-1]:
        start(("dz", k), dst_zsb.at[at_z(k)], dst_zrb.at[k - 1], dev(zz=at_z(k)))

    def back_x(e):
        for name, end, at, along in routes:
            block = end.at[c, at_x(nx - e), at(0)]
            arrived((name + "x", e, 0), block)
            for k in near:
                start((name + "x", e, k), block, block, along(k))

    def back_line(k):
        for name, end, at, along in routes:
            block = end.at[c, x, at(nz - k)]
            arrived((name, k), block)
            if k not in near:
                for e in range(1, nx):
                    start((name + "x", e, k), block, block, dev(xx=at_x(e)))

    back_x(1)
    back_x(nx - 1) if nx > 2 else None
    for k in far[:2]:
        back_line(k)
    for e in range(2, nx - 1):
        back_x(e)
    for k in [*far[2:], *near]:
        back_line(k)
    for name, end, at, along in routes:
        start((name + "c", 0), end.at[c, x], end.at[c, x], dev(cc=o))

    for e in range(1, nx):
        xx = at_x(nx - e)
        for name, end, at, along in routes:
            for k in range(1, nz):
                arrived((name + "x", e, k), end.at[c, xx, at(nz - k)])
            start((name + "c", e), end.at[c, xx], end.at[c, xx], dev(cc=o))

    def turn(half):
        lanes = pl.ds(pl.multiple_of(half * half_r, half_r), half_r)
        out_r[0:cut, lanes] = a_end[half].reshape(half_r, cut).T
        out_r[cut:, lanes] = b_end[half].reshape(half_r, width - cut).T

    turn(c)

    total = dst_zs[z]
    for k in range(1, nz):
        arrived(("dz", k), dst_zrb.at[k - 1])
        total = total + dst_zrb[k - 1].astype(F32)
    out_d[...] = total
    total = src_part[1, pl.ds(y * rows_s, rows_s), :]
    for k in range(1, ny):
        arrived(("ey", k), src_yr.at[k - 1])
        total = total + src_yr[k - 1].astype(F32)
    out_s[...] = total

    for e in range(nx):
        for name, end, at, along in routes:
            arrived((name + "c", e), end.at[o, at_x(nx - e)])
    turn(o)
    for d in live_copies:
        d.wait_send()
    assert len(slots) <= SEMS


def per_device(
    nz, nx, ny, src_table, dst_table, rel_diag, src_index, dst_index, rel_index, neg_index, edge_count
):
    rows_s, width = src_table.shape
    rows_d = dst_table.shape[0]
    n_rel = rel_diag.shape[0]
    rel_turned = rel_diag.T
    edges = src_index.shape[-1]
    spans, negs = neg_index.shape[2:]
    n_src, n_dst = ny * NC * rows_s, nz * nx * rows_d
    half_r = n_rel // NC
    quart_r = half_r // nx
    eighth_r = quart_r // ny
    cut = 256

    def v(shape, kind=F32):
        return pltpu.VMEM(shape, kind)

    grads = pl.pallas_call(
        functools.partial(kernel, nz, nx, ny),
        out_shape=(
            pltpu.VMEM((rows_s, width), F32),
            pltpu.VMEM((rows_d, width), F32),
            pltpu.VMEM((width, n_rel), F32),
        ),
        in_specs=[pl.BlockSpec(memory_space=pltpu.HBM)] * 7 + [pl.BlockSpec(memory_space=pltpu.VMEM)],
        out_specs=[pl.BlockSpec(memory_space=pltpu.VMEM)] * 3,
        scratch_shapes=[
            v((NC, ny, rows_s, width), BF16),
            v((nx, nz, rows_d, width), BF16),
            v((width, n_rel)),
            v((1, edges), I32),
            v((1, edges), I32),
            v((1, edges), I32),
            v((1, spans, negs), I32),
            v((edges, n_src), BF16),
            v((nx, edges, nz * rows_d), BF16),
            v((edges, n_rel), BF16),
            v((n_src, edges), BF16),
            v((n_dst, edges), BF16),
            v((n_rel, edges), BF16),
            v((spans, n_dst, 128)),
            v((edges, width)),
            v((edges, width)),
            v((edges, width)),
            v((edges, width)),
            v((edges, width)),
            v((edges, 128)),
            v((edges, width), BF16),
            v((nx, nz * rows_d, width)),
            v((2, half_r, width)),
            v((half_r, width)),
            v((nx - 1, quart_r, width), BF16),
            v((nx - 1, quart_r, width), BF16),
            *(
                v((*lead, eighth_r, wide))
                for wide in (cut, width - cut)
                for lead in ((ny,), (ny - 1,), (), (nz,), (NC, nx, ny))
            ),
            v((nx - 1, nz, rows_d, width), BF16),
            v((nz * rows_d, width)),
            v((nx - 1, nz, rows_d, width), BF16),
            v((nz, rows_d, width)),
            v((nz, rows_d, width), BF16),
            v((nz - 1, rows_d, width), BF16),
            v((2, ny * rows_s, width)),
            v((ny * rows_s, width)),
            v((ny - 1, rows_s, width), BF16),
            v((ny - 1, rows_s, width), BF16),
            pltpu.SemaphoreType.DMA((SEMS,)),
            pltpu.SemaphoreType.DMA((SEMS,)),
            pltpu.SemaphoreType.DMA((7,)),
        ],
        compiler_params=pltpu.CompilerParams(
            collective_id=0, has_side_effects=True, vmem_limit_bytes=50 * 1024 * 1024
        ),
    )(
        *(
            pltpu.with_memory_space_constraint(t, pltpu.HBM)
            for t in (src_table, dst_table, rel_turned, src_index[0], dst_index[0], rel_index[0], neg_index[0])
        ),
        edge_count,
    )
    return grads[0], grads[1], grads[2].T


def solution(mesh):
    sizes = dict(mesh.shape)
    return jax.shard_map(
        functools.partial(per_device, sizes["src"] // NX, NX, sizes["dst"] // NC),
        mesh=mesh,
        in_specs=(
            P(("src", "dst"), None),
            P(("dst", "src"), None),
            P(),
            P("src", "dst", None),
            P("src", "dst", None),
            P("src", "dst", None),
            P("src", "dst", None, None),
            P("src", "dst"),
        ),
        out_specs=(P(("src", "dst"), None), P(("dst", "src"), None), P()),
        check_vma=False,
    )
```

```python
import functools
import math

import jax
import jax.numpy as jnp
from jax import lax
from jax.experimental import pallas as pl
from jax.experimental.pallas import tpu as pltpu
from jax.sharding import PartitionSpec as P

F32, BF16, I32 = jnp.float32, jnp.bfloat16, jnp.int32
NX, NC = 4, 2
SEMS = 192


def dot(a, b):
    return jnp.dot(a, b, preferred_element_type=F32)


def dot_nt(a, b):
    return lax.dot_general(a, b, (((1,), (1,)), ((), ())), preferred_element_type=F32)


def split2(v):
    hi = v.astype(BF16)
    return hi, (v - hi.astype(F32)).astype(BF16)


def kernel(
    nz, nx, ny,
    src_hbm, dst_hbm, rel_hbm, si_hbm, di_hbm, ri_hbm, ni_hbm, cnt_ref,
    out_s, out_d, out_r,
    S, T, rel_v, si_ref, di_ref, ri_ref, ni_ref, hot_s, hot_d, hot_r, cold_s, cold_d, cold_r, counts, r_v, q_v, g_v, s_v, t_v, w_v, qb_v, spread,
    rel_part, rel_sib, rel_xs, rel_xr, a_first, a_got, a_mine, a_all, a_end, b_first, b_got, b_mine, b_all, b_end,
    dst_xs, dst_part, dst_xr, dst_zs, dst_zsb, dst_zrb,
    src_part, src_sib, src_ys, src_yr,
    send, recv, here,
):
    a, b = lax.axis_index("src"), lax.axis_index("dst")
    z, x = a // nx, lax.rem(a, nx)
    y, c = b // NC, lax.rem(b, NC)
    o = 1 - c
    rows_s, width = src_hbm.shape
    rows_d = dst_hbm.shape[0]
    half_s = ny * rows_s
    part_d = nz * rows_d
    n_dst = nx * part_d
    n_rel = rel_v.shape[1]
    half_r = n_rel // NC
    quart_r = half_r // nx
    near = sorted({1, nz - 1})
    cut = a_mine.shape[-1]
    assert ny == nz
    by_distance = sorted(range(1, nz), key=lambda k: min(k, nz - k))
    edges = si_ref.shape[-1]
    spans, negs = ni_ref.shape[-2], ni_ref.shape[-1]
    per = edges // spans
    inverse = 1.0 / math.sqrt(negs)

    def at_z(k):
        return lax.rem(z + k, nz)

    def at_x(k):
        return lax.rem(x + k, nx)

    def at_y(k):
        return lax.rem(y + k, ny)

    def dev(zz=z, xx=x, yy=y, cc=c):
        return (zz * nx + xx, yy * NC + cc)

    slots = {}
    live_copies = []

    def slot(key):
        return slots.setdefault(key, len(slots))

    def copy(key, src, dst, target):
        k = slot(key)
        return pltpu.make_async_remote_copy(
            src_ref=src, dst_ref=dst, send_sem=send.at[k], recv_sem=recv.at[k],
            device_id=target, device_id_type=pl.DeviceIdType.MESH,
        )

    def start(key, src, dst, target):
        d = copy(key, src, dst, target)
        d.start()
        live_copies.append(d)

    def arrived(key, dst):
        copy(key, dst, dst, dev(cc=o)).wait_recv()

    loads = [
        pltpu.make_async_copy(f, t, here.at[k])
        for k, (f, t) in enumerate(
            [
                (dst_hbm, T.at[x, z]), (src_hbm, S.at[c, y]), (ri_hbm, ri_ref), (si_hbm, si_ref),
                (di_hbm, di_ref), (rel_hbm, rel_v), (ni_hbm, ni_ref),
            ]
        )
    ]
    for d in loads:
        d.start()

    barrier = pltpu.get_barrier_semaphore()
    peers = [dev(cc=o)]
    peers += [dev(zz=at_z(k)) for k in range(1, nz)]
    peers += [dev(yy=at_y(k)) for k in range(1, ny)]
    peers += [dev(xx=at_x(k)) for k in range(1, nx)]
    for p in peers:
        pl.semaphore_signal(barrier, inc=1, device_id=p, device_id_type=pl.DeviceIdType.MESH)
    loads[0].wait()
    loads[1].wait()
    pl.semaphore_wait(barrier, len(peers))

    for e in range(1, nx):
        start(("tx", e, 0), T.at[x, z], T.at[x, z], dev(xx=at_x(e)))
    far = [k for k in by_distance if k not in near]
    for k in [*far, *near]:
        start(("tz", k), T.at[x, z], T.at[x, z], dev(zz=at_z(k)))
    for k in range(1, ny):
        start(("sy", k), S.at[c, y], S.at[c, y], dev(yy=at_y(k)))
    start(("sc", 0), S.at[c, y], S.at[c, y], dev(cc=o))

    for d in loads[2:]:
        d.wait()
    lx, ls = nx.bit_length() - 1, rows_s.bit_length() - 1

    def order_d(j):
        owner = (j * ((1 << 16) // rows_d + 1)) >> 16
        return j + ((owner & (nx - 1)) * nz + (owner >> lx) - owner) * rows_d

    si = si_ref[...]
    owner = si >> ls
    si = (si & (rows_s - 1)) + (owner & 1) * half_s + (owner >> 1) * rows_s
    di = order_d(di_ref[...])
    ri = ri_ref[...]
    number = lax.broadcasted_iota(I32, (1, edges), 1)
    live_row = jnp.where(number < cnt_ref[...], 1.0, 0.0).astype(F32)
    columns = jnp.concatenate(
        [si.astype(F32), di.astype(F32), ri.astype(F32), live_row, jnp.zeros((4, edges), F32)], axis=0
    ).T
    si_c, di_c, ri_c = (columns[:, k : k + 1].astype(I32) for k in range(3))
    live_col = columns[:, 3:4]

    def hot(index, shape, dim):
        return jnp.where(index == lax.broadcasted_iota(I32, shape, dim), 1.0, 0.0).astype(BF16)

    def forward_z(k):
        zz = at_z(nz - k)
        arrived(("tz", k), T.at[x, zz])
        for e in range(1, nx):
            start(("tx", e, k), T.at[x, zz], T.at[x, zz], dev(xx=at_x(e)))

    def forward_x(e):
        xx = at_x(nx - e)
        arrived(("tx", e, 0), T.at[xx, z])
        for k in near:
            start(("tx", e, k), T.at[xx, z], T.at[xx, z], dev(zz=at_z(k)))

    def forward_y(k):
        yy = at_y(ny - k)
        arrived(("sy", k), S.at[c, yy])
        start(("sc", k), S.at[c, yy], S.at[c, yy], dev(cc=o))

    hot_r[...] = hot(ri_c, (edges, n_rel), 1)
    hot_s[...] = hot(si_c, (edges, NC * half_s), 1)
    forward_x(1)
    forward_x(nx - 1) if nx > 2 else None
    for k in far[:2]:
        forward_z(k)
    rel = rel_v[...]
    r1, r2 = split2(rel)
    r3 = (rel - r1.astype(F32) - r2.astype(F32)).astype(BF16)
    hr = hot_r[...]
    r_v[...] = dot_nt(hr, r1) + dot_nt(hr, r2) + dot_nt(hr, r3)
    for e in range(2, nx - 1):
        forward_x(e)
    for k in far[2:]:
        forward_z(k)
    for k in range(1, ny):
        forward_y(k)
    for e in range(nx):
        hot_d[e] = hot(di_c - at_x(nx - e) * part_d, (edges, part_d), 1)

    ones = jnp.ones((negs, 128), BF16)
    for m in range(spans):
        nidx = order_d(ni_ref[0, m : m + 1, :])
        counts[m] = dot(hot(nidx, (n_dst, negs), 0), ones)
    cold_r[...] = hot(ri, (n_rel, edges), 0)

    for k in range(ny):
        arrived(("sc", k), S.at[o, at_y(ny - k)])
    table_s = S[...].reshape(NC * half_s, width)
    s = dot(hot_s[...], table_s)
    s_v[...] = s
    q = s * r_v[...]
    q_v[...] = q
    qb_v[...] = q.astype(BF16)

    def weights(live, scores):
        return (live * jax.nn.sigmoid(scores) * inverse).astype(BF16)

    def spread_terms(xx):
        part = pl.ds(xx * part_d, part_d)
        tab = T[xx].reshape(part_d, width)
        total = jnp.zeros((part_d, width), F32)
        for m in range(spans):
            qb = qb_v[pl.ds(m * per, per), :]
            wn = weights(live_row[:, m * per : (m + 1) * per], dot_nt(tab, qb))
            total = total + counts[m, part, 0:1] * dot(wn, qb)
        spread[xx] = total

    arrivals = [0, *sorted(range(1, nx), key=lambda e: min(e, nx - e))]
    for n, e in enumerate(arrivals):
        xx = at_x(nx - e)
        if e == 0:
            for k in near:
                arrived(("tz", k), T.at[x, at_z(nz - k)])
        else:
            for k in range(1, nz):
                arrived(("tx", e, k), T.at[xx, at_z(nz - k)])
        tab = T[xx].reshape(part_d, width)
        t = dot(hot_d[e], tab)
        t_v[...] = t if n == 0 else t_v[...] + t
        tab_f = tab.astype(F32)
        for m in range(spans):
            span = pl.ds(m * per, per)
            uh, ul = split2(tab_f * counts[m, pl.ds(xx * part_d, part_d), 0:1])
            wn = weights(live_col[m * per : (m + 1) * per], dot_nt(qb_v[span, :], tab))
            pulled = dot(wn, uh) + dot(wn, ul)
            g_v[span, :] = pulled if n == 0 else g_v[span, :] + pulled
        if n == 0:
            spread_terms(xx)
    p = jnp.sum(q_v[...] * t_v[...], axis=1, keepdims=True)
    w = -live_col * jax.nn.sigmoid(-p)
    w_v[...] = jnp.broadcast_to(w, w_v.shape)
    g_v[...] = w * t_v[...] + g_v[...]

    sg = s_v[...] * g_v[...]
    h, l = split2(sg)
    theirs = cold_r[pl.ds(o * half_r, half_r), :]
    rel_part[0] = dot(theirs, h) + dot(theirs, l)
    order_x = [*range(nx // 2, 0, -1), *range(nx // 2 + 1, nx)]

    def quarter(e):
        return pl.ds(at_x(e) * quart_r, quart_r)

    for e in [*order_x, 0]:
        start(("rc", e), rel_part.at[0, quarter(e)], rel_sib.at[quarter(e)], dev(cc=o))
    mine = cold_r[pl.ds(c * half_r, half_r), :]
    rel_part[1] = dot(mine, h) + dot(mine, l)

    for e in order_x:
        arrived(("rc", e), rel_sib.at[quarter(e)])
        rel_xs[e - 1] = (rel_part[1, quarter(e), :] + rel_sib[quarter(e), :]).astype(BF16)
        start(("rx", e), rel_xs.at[e - 1], rel_xr.at[e - 1], dev(xx=at_x(e)))

    cold_d[...] = hot(di, (n_dst, edges), 0)
    wh, wl = split2(w_v[:, 0:1] * q_v[...])

    def target_terms(e):
        xx = at_x(e)
        cd = cold_d[pl.ds(xx * part_d, part_d), :]
        total = dot(cd, wh) + dot(cd, wl) + spread[xx]
        if e == 0:
            dst_part[...] = total
        else:
            dst_xs[e - 1] = total.astype(BF16).reshape(nz, rows_d, width)
            start(("dx", e), dst_xs.at[e - 1], dst_xr.at[e - 1], dev(xx=xx))

    for e in range(1, nx):
        spread_terms(at_x(e))
        target_terms(e)

    cold_s[...] = hot(si, (NC * half_s, edges), 0)
    sh, sl = split2(r_v[...] * g_v[...])
    theirs = cold_s[pl.ds(o * half_s, half_s), :]
    src_part[0] = dot(theirs, sh) + dot(theirs, sl)
    start(("ec",), src_part.at[0], src_sib, dev(cc=o))

    arrived(("rc", 0), rel_sib.at[quarter(0)])
    total = rel_part[1, quarter(0), :] + rel_sib[quarter(0), :]
    for e in range(1, nx):
        arrived(("rx", e), rel_xr.at[e - 1])
        total = total + rel_xr[e - 1].astype(F32)
    a_first[...] = total[:, :cut].reshape(a_first.shape)
    b_first[...] = total[:, cut:].reshape(b_first.shape)
    for k in range(1, ny):
        start(("ay", k), a_first.at[at_y(k)], a_got.at[k - 1], dev(yy=at_y(k)))
        start(("bz", k), b_first.at[at_z(k)], b_got.at[k - 1], dev(zz=at_z(k)))

    mine = cold_s[pl.ds(c * half_s, half_s), :]
    src_part[1] = dot(mine, sh) + dot(mine, sl)
    arrived(("ec",), src_sib)
    src_part[1] = src_part[1] + src_sib[...]
    for k in range(1, ny):
        src_ys[k - 1] = src_part[1, pl.ds(at_y(k) * rows_s, rows_s), :].astype(BF16)
    target_terms(0)

    ta, tb = a_first[y], b_first[z]
    for k in range(1, ny):
        arrived(("ay", k), a_got.at[k - 1])
        ta = ta + a_got[k - 1]
    a_mine[...] = ta
    for k in range(1, nz):
        start(("az", k), a_mine, a_all.at[k - 1], dev(zz=at_z(k)))
    for k in range(1, nz):
        arrived(("bz", k), b_got.at[k - 1])
        tb = tb + b_got[k - 1]
    b_mine[...] = tb
    for k in range(1, ny):
        start(("by", k), b_mine, b_all.at[k - 1], dev(yy=at_y(k)))
    a_all[nz - 1] = ta
    b_all[ny - 1] = tb

    for k in range(1, ny):
        start(("ey", k), src_ys.at[k - 1], src_yr.at[k - 1], dev(yy=at_y(k)))

    for k in range(1, nz):
        arrived(("az", k), a_all.at[k - 1])
    total = jnp.zeros(a_mine.shape, F32)
    for zz in range(nz):
        total = total + a_all[lax.rem(z - zz + 2 * nz - 1, nz)]
    a_end[c, x, y] = total
    for k in range(1, ny):
        arrived(("by", k), b_all.at[k - 1])
    total = jnp.zeros(b_mine.shape, F32)
    for yy in range(ny):
        total = total + b_all[lax.rem(y - yy + 2 * ny - 1, ny)]
    b_end[c, x, z] = total

    def along_y(k):
        return dev(yy=at_y(k))

    def along_z(k):
        return dev(zz=at_z(k))

    routes = [("A", a_end, at_y, along_y), ("B", b_end, at_z, along_z)]
    def back_own(k):
        for name, end, at, along in routes:
            start((name, k), end.at[c, x, at(0)], end.at[c, x, at(0)], along(k))

    for k in far[::-1]:
        back_own(k)
    for e in range(1, nx):
        for name, end, at, along in routes:
            start((name + "x", e, 0), end.at[c, x, at(0)], end.at[c, x, at(0)], dev(xx=at_x(e)))
    for k in near:
        back_own(k)

    for e in range(1, nx):
        arrived(("dx", e), dst_xr.at[e - 1])
    total = dst_part[...]
    for e in range(1, nx):
        total = total + dst_xr[e - 1].astype(F32).reshape(part_d, width)
    dst_zs[...] = total.reshape(dst_zs.shape)
    dst_zsb[...] = dst_zs[...].astype(BF16)

    for k in by_distance[::-1]:
        start(("dz", k), dst_zsb.at[at_z(k)], dst_zrb.at[k - 1], dev(zz=at_z(k)))

    def back_x(e):
        for name, end, at, along in routes:
            block = end.at[c, at_x(nx - e), at(0)]
            arrived((name + "x", e, 0), block)
            for k in near:
                start((name + "x", e, k), block, block, along(k))

    def back_line(k):
        for name, end, at, along in routes:
            block = end.at[c, x, at(nz - k)]
            arrived((name, k), block)
            if k not in near:
                for e in range(1, nx):
                    start((name + "x", e, k), block, block, dev(xx=at_x(e)))

    back_x(1)
    back_x(nx - 1) if nx > 2 else None
    for k in far[:2]:
        back_line(k)
    for e in range(2, nx - 1):
        back_x(e)
    for k in [*far[2:], *near]:
        back_line(k)
    for name, end, at, along in routes:
        start((name + "c", 0), end.at[c, x], end.at[c, x], dev(cc=o))

    for e in range(1, nx):
        xx = at_x(nx - e)
        for name, end, at, along in routes:
            for k in range(1, nz):
                arrived((name + "x", e, k), end.at[c, xx, at(nz - k)])
            start((name + "c", e), end.at[c, xx], end.at[c, xx], dev(cc=o))

    def turn(half):
        lanes = pl.ds(pl.multiple_of(half * half_r, half_r), half_r)
        out_r[0:cut, lanes] = a_end[half].reshape(half_r, cut).T
        out_r[cut:, lanes] = b_end[half].reshape(half_r, width - cut).T

    turn(c)

    total = dst_zs[z]
    for k in range(1, nz):
        arrived(("dz", k), dst_zrb.at[k - 1])
        total = total + dst_zrb[k - 1].astype(F32)
    out_d[...] = total
    total = src_part[1, pl.ds(y * rows_s, rows_s), :]
    for k in range(1, ny):
        arrived(("ey", k), src_yr.at[k - 1])
        total = total + src_yr[k - 1].astype(F32)
    out_s[...] = total

    for e in range(nx):
        for name, end, at, along in routes:
            arrived((name + "c", e), end.at[o, at_x(nx - e)])
    turn(o)
    for d in live_copies:
        d.wait_send()
    assert len(slots) <= SEMS


def per_device(
    nz, nx, ny, src_table, dst_table, rel_diag, src_index, dst_index, rel_index, neg_index, edge_count
):
    rows_s, width = src_table.shape
    rows_d = dst_table.shape[0]
    n_rel = rel_diag.shape[0]
    rel_turned = rel_diag.T
    edges = src_index.shape[-1]
    spans, negs = neg_index.shape[2:]
    n_src, n_dst = ny * NC * rows_s, nz * nx * rows_d
    half_r = n_rel // NC
    quart_r = half_r // nx
    eighth_r = quart_r // ny
    cut = 256

    def v(shape, kind=F32):
        return pltpu.VMEM(shape, kind)

    grads = pl.pallas_call(
        functools.partial(kernel, nz, nx, ny),
        out_shape=(
            pltpu.VMEM((rows_s, width), F32),
            pltpu.VMEM((rows_d, width), F32),
            pltpu.VMEM((width, n_rel), F32),
        ),
        in_specs=[pl.BlockSpec(memory_space=pltpu.HBM)] * 7 + [pl.BlockSpec(memory_space=pltpu.VMEM)],
        out_specs=[pl.BlockSpec(memory_space=pltpu.VMEM)] * 3,
        scratch_shapes=[
            v((NC, ny, rows_s, width), BF16),
            v((nx, nz, rows_d, width), BF16),
            v((width, n_rel)),
            v((1, edges), I32),
            v((1, edges), I32),
            v((1, edges), I32),
            v((1, spans, negs), I32),
            v((edges, n_src), BF16),
            v((nx, edges, nz * rows_d), BF16),
            v((edges, n_rel), BF16),
            v((n_src, edges), BF16),
            v((n_dst, edges), BF16),
            v((n_rel, edges), BF16),
            v((spans, n_dst, 128)),
            v((edges, width)),
            v((edges, width)),
            v((edges, width)),
            v((edges, width)),
            v((edges, width)),
            v((edges, 128)),
            v((edges, width), BF16),
            v((nx, nz * rows_d, width)),
            v((2, half_r, width)),
            v((half_r, width)),
            v((nx - 1, quart_r, width), BF16),
            v((nx - 1, quart_r, width), BF16),
            *(
                v((*lead, eighth_r, wide))
                for wide in (cut, width - cut)
                for lead in ((ny,), (ny - 1,), (), (nz,), (NC, nx, ny))
            ),
            v((nx - 1, nz, rows_d, width), BF16),
            v((nz * rows_d, width)),
            v((nx - 1, nz, rows_d, width), BF16),
            v((nz, rows_d, width)),
            v((nz, rows_d, width), BF16),
            v((nz - 1, rows_d, width), BF16),
            v((2, ny * rows_s, width)),
            v((ny * rows_s, width)),
            v((ny - 1, rows_s, width), BF16),
            v((ny - 1, rows_s, width), BF16),
            pltpu.SemaphoreType.DMA((SEMS,)),
            pltpu.SemaphoreType.DMA((SEMS,)),
            pltpu.SemaphoreType.DMA((7,)),
        ],
        compiler_params=pltpu.CompilerParams(
            collective_id=0, has_side_effects=True, vmem_limit_bytes=50 * 1024 * 1024
        ),
    )(
        *(
            pltpu.with_memory_space_constraint(t, pltpu.HBM)
            for t in (src_table, dst_table, rel_turned, src_index[0], dst_index[0], rel_index[0], neg_index[0])
        ),
        edge_count,
    )
    return grads[0], grads[1], grads[2].T


def solution(mesh):
    sizes = dict(mesh.shape)
    return jax.shard_map(
        functools.partial(per_device, sizes["src"] // NX, NX, sizes["dst"] // NC),
        mesh=mesh,
        in_specs=(
            P(("src", "dst"), None),
            P(("dst", "src"), None),
            P(),
            P("src", "dst", None),
            P("src", "dst", None),
            P("src", "dst", None),
            P("src", "dst", None, None),
            P("src", "dst"),
        ),
        out_specs=(P(("src", "dst"), None), P(("dst", "src"), None), P()),
        check_vma=False,
    )
```
